128 devices in a mesh: dp: 32 (over x, y, core), tensor: 4 (over z).
Axes of the slice: x: 4, y: 4, z: 4, core: 2. Of those that a mesh axis runs over, the one named last changes fastest.
Arguments:
- hidden: bfloat16 [16384, 8192], P('dp', 'tensor'), may hold values from -6 to 6
- key_weight_frozen: bfloat16 [8192, 1024], P(None, 'tensor'), may hold values from -0.0625 to 0.0625
- value_weight_frozen: bfloat16 [8192, 1024], P(None, 'tensor'), may hold values from -0.0625 to 0.0625
- adapter_down_maps: bfloat16 [64, 2, 16, 8192], P('dp', None, None, 'tensor'), may hold values from -0.0625 to 0.0625
- adapter_up_maps: bfloat16 [64, 2, 16, 1024], P('dp', None, None, 'tensor'), may hold values from -0.375 to 0.375
- block_adapter_index: int32 [128], P('dp'), may hold values from 0 to 63
- segment_document_index: int32 [32, 512], P('dp'), may hold values from 0 to 15, never falling along the last dimension, each value on 1 to 256 neighbouring positions
- adapter_position: int32 [64], replicated, may hold values from 0 to 63, each once
- key_gradient: bfloat16 [16384, 1024], P('dp', 'tensor'), may hold values from -1.5 to 1.5
- value_gradient: bfloat16 [16384, 1024], P('dp', 'tensor'), may hold values from -1.5 to 1.5
Outputs:
- key_out: bfloat16 [16384, 1024], P('dp', 'tensor')
- value_output: bfloat16 [16384, 1024], P('dp', 'tensor')
- hidden_gradient: bfloat16 [16384, 8192], P('dp', 'tensor')
- grad_down: float32 [64, 2, 16, 8192], P('dp', None, None, 'tensor')
- grad_up: float32 [64, 2, 16, 1024], P('dp', None, None, 'tensor')
The draws below stay inside these ranges and needn't reach their ends.
Inputs may be any that keep to these rules, and one draw needn't show every extreme that they name: `block_adapter_index`: adapter of each block of 128 tokens. `segment_document_index`: in each row, document numbers never fall, each document has 1 to 256 tokens and one has exactly 256. A permutation: adapter a's weights and gradients sit at index adapter_position[a] of adapter_down_maps, adapter_up_maps, grad_down and grad_up.
All inputs are finite; a program needn't handle non-finite values.
Results may differ from the reference program's by a relative error of at most 0.022.
Values may be sent and summed in bfloat16 or wider, within the bound.
No kernel may reach another device: no remote copies, remote signals or barrier semaphores. Data moves between devices by JAX's collectives and lax.ppermute only.
A program may use at most 192 MiB of HBM per device.

```python
import math
import jax
import jax.numpy as jnp
import numpy as np
from jax import lax

MODEL_WIDTH = 8192
KVH = 8
HEAD = 128
ADAPTER_RANK = 16
BLOCK = 128
TOK_DEV = 512
KEY_VALUE_WIDTH = 1024
ADAPTER_TOTAL = 64
TOKEN_TOTAL = 16384
BLOCKS = 128
DOCS = 16
N_DP = 32


def touch_ends(drawn, own_key, smallest, largest):
    extent = drawn.shape
    place = [jax.random.randint(jax.random.fold_in(own_key, axis), (), 0, extent[axis]) for axis in range(len(extent))]
    drawn = drawn.at[tuple(place)].set(smallest)
    longest = extent.index(max(extent))
    place[longest] = (place[longest] + 1) % extent[longest]
    return drawn.at[tuple(place)].set(largest)


def block_levels(own_key, shape, cuts, least, top_value):
    def one(axis_at, shards_of):
        draws = jax.random.uniform(jax.random.fold_in(jax.random.fold_in(own_key, 6), axis_at), (shards_of,), jnp.float32, least / len(cuts), top_value / len(cuts))
        return jnp.repeat(jnp.exp(draws), shape[axis_at] // shards_of).reshape((-1,) + (1,) * (len(shape) - axis_at - 1))

    level = one(*cuts[0])
    for cut in cuts[1:]:
        level = level * one(*cut)
    return level


def cumulative_ranks(number_of, slope):
    loads = [(1 << 20) // math.isqrt(standing ** slope) + 1 for standing in range(1, number_of + 1)]
    deviation = 1 + sum(loads) // (1 << 30)
    return np.cumsum(np.array([max(1, weight // deviation) for weight in loads]))


def ranked(own_key, shape, number_of, skew):
    grid = cumulative_ranks(number_of, skew)
    lot = jax.random.randint(jax.random.fold_in(own_key, 1), shape, 0, int(grid[number_of - 1]))
    grade = jnp.searchsorted(jnp.asarray(grid, jnp.int32), lot, side="right")
    return jax.random.permutation(jax.random.fold_in(own_key, 2), number_of)[grade].astype(jnp.int32)


def length_profile(number_of, total, reach, slope):
    portions = [(1 << 20) // math.isqrt(standing ** slope) + 1 for standing in range(2, number_of + 1)]
    surplus, counts = total - reach - (number_of - 1), [1] * (number_of - 1)
    while surplus > 0:
        movable = [i for i in range(number_of - 1) if counts[i] < reach]
        whole, left = sum([portions[i] for i in movable]), surplus
        for i in movable:
            extra = min(reach - counts[i], max(1, left * portions[i] // whole), surplus)
            counts[i] = counts[i] + extra
            surplus = surplus - extra
    return np.array([reach] + counts)


def ragged(rng, number_of, total, reach, slope):
    if number_of == 2:
        one = jax.random.randint(rng, (), max(1, total - reach), min(reach, total - 1) + 1)
        return jnp.stack([one, total - one])
    lengths = jnp.asarray(length_profile(number_of, total, reach, slope), jnp.int32)
    pairs = (number_of - 1) // 2
    source_of, sink = lengths[1:1 + 2 * pairs:2], lengths[2:2 + 2 * pairs:2]
    slack = jnp.minimum(source_of - 1, reach - sink)
    moved = jax.random.randint(jax.random.fold_in(rng, 1), (pairs,), 0, 1 << 20) % (slack + 1)
    lengths = lengths.at[1:1 + 2 * pairs:2].set(source_of - moved).at[2:2 + 2 * pairs:2].set(sink + moved)
    return lengths[jax.random.permutation(jax.random.fold_in(rng, 2), number_of)]


def noise(key, shape, spread, reach, cuts=(), kind=jnp.bfloat16):
    values = spread * jax.random.normal(key, shape, jnp.float32)
    if cuts:
        values = values * block_levels(key, shape, cuts, -0.22, 0.18)
    return jnp.clip(values, -reach, reach).astype(kind)


def setup_inputs(seed: int = 0) -> dict:
    splits = jax.random.split(jax.random.key(seed), 11)
    return {
        "hidden": noise(splits[0], (TOKEN_TOTAL, MODEL_WIDTH), 1.0, 6.0, ((0, 32), (1, 4))),
        "key_weight_frozen": noise(splits[1], (MODEL_WIDTH, KEY_VALUE_WIDTH), MODEL_WIDTH ** -0.5, 0.0625, ((1, 4),)),
        "value_weight_frozen": noise(splits[2], (MODEL_WIDTH, KEY_VALUE_WIDTH), MODEL_WIDTH ** -0.5, 0.0625, ((1, 4),)),
        "adapter_down_maps": noise(splits[3], (ADAPTER_TOTAL, 2, ADAPTER_RANK, MODEL_WIDTH), MODEL_WIDTH ** -0.5, 0.0625, ((0, 32), (3, 4))),
        "adapter_up_maps": noise(splits[4], (ADAPTER_TOTAL, 2, ADAPTER_RANK, KEY_VALUE_WIDTH), (16 * ADAPTER_RANK) ** -0.5, 0.375, ((0, 32), (3, 4))),
        "block_adapter_index": touch_ends(ranked(splits[5], (BLOCKS,), ADAPTER_TOTAL, 2), jax.random.fold_in(splits[5], 3), 0, ADAPTER_TOTAL - 1).astype(jnp.int32),
        "segment_document_index": jax.vmap(lambda own: jnp.searchsorted(jnp.cumsum(ragged(own, DOCS, TOK_DEV, TOK_DEV // 2, 1)), jnp.arange(TOK_DEV), side="right"))(jax.random.split(splits[6], N_DP)).reshape((N_DP, TOK_DEV)).astype(jnp.int32),
        "adapter_position": jax.random.permutation(splits[7], ADAPTER_TOTAL).astype(jnp.int32),
        "key_gradient": noise(splits[8], (TOKEN_TOTAL, KEY_VALUE_WIDTH), 0.25, 1.5, ((0, 32), (1, 4))),
        "value_gradient": noise(splits[9], (TOKEN_TOTAL, KEY_VALUE_WIDTH), 0.25, 1.5, ((0, 32), (1, 4))),
    }


adapter_scale = 0.5
rope_theta = 500000.0


def rope_tables(segments):
    places = jnp.arange(segments.shape[1], dtype=jnp.int32)
    earlier = jnp.concatenate([segments[:, :1] - 1, segments[:, :-1]], axis=1)
    starts = lax.cummax(jnp.where(segments != earlier, places[None, :], 0), axis=1)
    position = (places[None, :] - starts).astype(jnp.float32).reshape(-1)
    halves = jnp.arange(HEAD // 2, dtype=jnp.float32)
    inverse = jnp.exp(halves * (-2.0 * math.log(rope_theta) / HEAD))
    angles = position[:, None] * inverse[None, :]
    return jnp.cos(angles), jnp.sin(angles)


def rotate(values, cosine, sine):
    leading = values[..., : HEAD // 2]
    trailing = values[..., HEAD // 2:]
    cosine = cosine[:, None, :]
    sine = sine[:, None, :]
    return jnp.concatenate([leading * cosine - trailing * sine, trailing * cosine + leading * sine], axis=-1)


def unrotate(values, cosine, sine):
    leading = values[..., : HEAD // 2]
    trailing = values[..., HEAD // 2:]
    cosine = cosine[:, None, :]
    sine = sine[:, None, :]
    return jnp.concatenate([leading * cosine + trailing * sine, trailing * cosine - leading * sine], axis=-1)


def reference(hidden, key_weight_frozen, value_weight_frozen, adapter_down_maps, adapter_up_maps, block_adapter_index, segment_document_index, adapter_position, key_gradient, value_gradient):
    cosine, sine = rope_tables(segment_document_index)
    slot_index_list = jnp.take(adapter_position, block_adapter_index, axis=0).astype(jnp.int32)
    block_down_maps = jnp.take(adapter_down_maps, slot_index_list, axis=0).astype(jnp.float32)
    block_up_maps = jnp.take(adapter_up_maps, slot_index_list, axis=0).astype(jnp.float32)
    blocked_tokens = hidden.reshape(BLOCKS, BLOCK, MODEL_WIDTH).astype(jnp.float32)
    adapter_input = jnp.einsum('qli,qogi->qlog', blocked_tokens, block_down_maps).astype(jnp.bfloat16)
    adapter_added_output = jnp.einsum('ezwp,ewpu->ezwu', adapter_input.astype(jnp.float32), block_up_maps).reshape(TOKEN_TOTAL, 2, KEY_VALUE_WIDTH) * adapter_scale
    key_before_adapter = jnp.dot(hidden, key_weight_frozen, preferred_element_type=jnp.float32) + adapter_added_output[:, 0]
    value_before_adapter = jnp.dot(hidden, value_weight_frozen, preferred_element_type=jnp.float32) + adapter_added_output[:, 1]
    key_out = rotate(key_before_adapter.reshape(TOKEN_TOTAL, KVH, HEAD), cosine, sine).reshape(TOKEN_TOTAL, KEY_VALUE_WIDTH).astype(jnp.bfloat16)
    value_output = value_before_adapter.astype(jnp.bfloat16)
    key_back = unrotate(key_gradient.astype(jnp.float32).reshape(TOKEN_TOTAL, KVH, HEAD), cosine, sine).reshape(TOKEN_TOTAL, KEY_VALUE_WIDTH).astype(jnp.bfloat16)
    backward_terms = jnp.stack([key_back, value_gradient], axis=1).reshape(BLOCKS, BLOCK, 2, KEY_VALUE_WIDTH).astype(jnp.float32)
    inner_gradient = (jnp.einsum('oezl,ozal->oeza', backward_terms, block_up_maps) * adapter_scale).astype(jnp.bfloat16)
    dims = (((1,), (1,)), ((), ()))
    frozen_output = lax.dot_general(key_back, key_weight_frozen, dims, preferred_element_type=jnp.float32)
    frozen_output = frozen_output + lax.dot_general(value_gradient, value_weight_frozen, dims, preferred_element_type=jnp.float32)
    adapter_backward = jnp.einsum('qvtx,qtxm->qvm', inner_gradient.astype(jnp.float32), block_down_maps).reshape(TOKEN_TOTAL, MODEL_WIDTH)
    hidden_gradient = (frozen_output + adapter_backward).astype(jnp.bfloat16)
    part_down = jnp.einsum('nbjr,nbd->njrd', inner_gradient.astype(jnp.float32), blocked_tokens)
    partial_up_map = jnp.einsum('qwth,qwtm->qthm', adapter_input.astype(jnp.float32), backward_terms) * adapter_scale
    per_group = TOK_DEV // BLOCK
    onehot_all = (slot_index_list.reshape(N_DP, per_group)[:, :, None] == jnp.arange(ADAPTER_TOTAL, dtype=jnp.int32)[None, None, :]).astype(jnp.float32)

    def group_sum(totals, index):
        onehot = lax.dynamic_index_in_dim(onehot_all, index, 0, keepdims=False)
        piece_down = lax.dynamic_slice_in_dim(part_down, index * per_group, per_group, 0)
        piece_up = lax.dynamic_slice_in_dim(partial_up_map, index * per_group, per_group, 0)
        dense_down = jnp.einsum('na,njrd->ajrd', onehot, piece_down, precision=lax.Precision.HIGHEST)
        dense_up = jnp.einsum('na,njrk->ajrk', onehot, piece_up, precision=lax.Precision.HIGHEST)
        dense_down = lax.optimization_barrier(dense_down.astype(jnp.bfloat16)).astype(jnp.float32)
        dense_up = lax.optimization_barrier(dense_up.astype(jnp.bfloat16)).astype(jnp.float32)
        return (totals[0] + dense_down, totals[1] + dense_up), None

    start_down = jnp.zeros((ADAPTER_TOTAL, 2, ADAPTER_RANK, MODEL_WIDTH), jnp.float32)
    start_up = jnp.zeros((ADAPTER_TOTAL, 2, ADAPTER_RANK, KEY_VALUE_WIDTH), jnp.float32)
    (grad_down, grad_up), unused = lax.scan(group_sum, (start_down, start_up), jnp.arange(N_DP, dtype=jnp.int32))
    return key_out, value_output, hidden_gradient, grad_down, grad_up
```

```python
import math

import jax
import jax.numpy as jnp
from jax import lax
from jax.experimental import pallas as pl
from jax.experimental.pallas import tpu as pltpu
from jax.sharding import PartitionSpec as P

HEAD = 128
SIDE = 4
SHIFTS = (1, -1, 2)

adapter_scale = 0.5
rope_theta = 500000.0
bf16 = jnp.bfloat16
f32 = jnp.float32
ANY = pl.BlockSpec(memory_space=pl.ANY)
VMEM = pl.BlockSpec(memory_space=pltpu.VMEM)
SMEM = pl.BlockSpec(memory_space=pltpu.SMEM)
NT = (((1,), (1,)), ((), ()))
TN = (((0,), (0,)), ((), ()))


def exchange(array, move):
    pairs = []
    for x in range(SIDE):
        for y in range(SIDE):
            for c in range(2):
                for z in range(SIDE):
                    x2, y2, c2, z2 = move(x, y, c, z)
                    target = (((x2 % SIDE) * SIDE + y2 % SIDE) * 2 + c2) * SIDE + z2 % SIDE
                    pairs.append((((x * SIDE + y) * 2 + c) * SIDE + z, target))
    return lax.ppermute(array, ("dp", "tensor"), pairs)


def along_z(array, shift):
    return exchange(array, lambda x, y, c, z: (x, y, c, z + shift))


def to_other_core(array):
    return exchange(array, lambda x, y, c, z: (x, y, 1 - c, z))


def along_line(array, shift):
    return exchange(
        array, lambda x, y, c, z: (x + shift, y, c, z) if c == 0 else (x, y + shift, c, z)
    )


def along_cross(array, shift):
    return exchange(
        array, lambda x, y, c, z: (x, y + shift, c, z) if c == 0 else (x + shift, y, c, z)
    )


def params(megabytes):
    return pltpu.CompilerParams(vmem_limit_bytes=megabytes << 20)


def cost(flops, moved):
    return pl.CostEstimate(flops=flops, bytes_accessed=moved, transcendentals=0)


def rope_tables(segments):
    places = jnp.arange(segments.shape[1], dtype=jnp.int32)
    earlier = jnp.concatenate([segments[:, :1] - 1, segments[:, :-1]], axis=1)
    starts = lax.cummax(jnp.where(segments != earlier, places[None, :], 0), axis=1)
    position = (places[None, :] - starts).astype(jnp.float32).reshape(-1)
    halves = jnp.arange(HEAD // 2, dtype=jnp.float32)
    inverse = jnp.exp(halves * (-2.0 * math.log(rope_theta) / HEAD))
    angles = position[:, None] * inverse[None, :]
    return (jnp.cos(angles), jnp.sin(angles))


def rotate(values, cosine, sine):
    leading = values[..., : HEAD // 2]
    trailing = values[..., HEAD // 2 :]
    cosine = cosine[:, None, :]
    sine = sine[:, None, :]
    return jnp.concatenate(
        [leading * cosine - trailing * sine, trailing * cosine + leading * sine], axis=-1
    )


def unrotate(values, cosine, sine):
    leading = values[..., : HEAD // 2]
    trailing = values[..., HEAD // 2 :]
    cosine = cosine[:, None, :]
    sine = sine[:, None, :]
    return jnp.concatenate(
        [leading * cosine + trailing * sine, trailing * cosine - leading * sine], axis=-1
    )


def pick_kernel(index, place, own, one, minus, two, *rest):
    outs, line, load, save = rest[:4], rest[4], rest[5], rest[6]
    n = own.shape[0]
    loads = []
    for i, source in enumerate((own, one, minus, two)):
        copy = pltpu.make_async_copy(source, line.at[pl.ds(place[i] * n, n)], load.at[i])
        copy.start()
        loads.append(copy)
    for copy in loads:
        copy.wait()
    saves = []
    for i in range(4):
        for b in range(n):
            copy = pltpu.make_async_copy(
                line.at[index[i * n + b]], outs[i].at[b], save.at[i * n + b]
            )
            copy.start()
            saves.append(copy)
    for copy in saves:
        copy.wait()


def pick(index, place, pieces):
    shape = pieces[0].shape
    return pl.pallas_call(
        pick_kernel,
        out_shape=[jax.ShapeDtypeStruct(shape, bf16)] * 4,
        in_specs=[SMEM, SMEM] + [ANY] * 4,
        out_specs=[ANY] * 4,
        scratch_shapes=[
            pltpu.VMEM((4 * shape[0],) + shape[1:], bf16),
            pltpu.SemaphoreType.DMA((4,)),
            pltpu.SemaphoreType.DMA((4 * shape[0],)),
        ],
        compiler_params=params(16),
        cost_estimate=cost(0, 16 * pieces[0].size),
    )(index, place, *pieces)


def lora_kernel(origin, hidden, key_back, value_back, s0, s1, s2, s3, out, maps, sems):
    blocks, both, wide = maps.shape
    width = hidden.shape[1]
    tokens = hidden.shape[0] // blocks
    for b in range(blocks):
        for i, source in enumerate((s0, s1, s2, s3)):

            @pl.when(origin[b] == i)
            def _():
                pltpu.make_async_copy(source.at[b], maps.at[b], sems.at[b]).start()

    half = lax.broadcasted_iota(jnp.int32, (both, tokens), 0) < both // 2
    for b in range(blocks):
        pltpu.make_async_copy(s0.at[b], maps.at[b], sems.at[b]).wait()
        rows = pl.ds(b * tokens, tokens)
        down = maps[b, :, :width]
        up = maps[b, :, width:]
        into = lax.dot_general(down, hidden[rows, :], NT, preferred_element_type=f32)
        keys = lax.dot_general(up, key_back[rows, :], NT, preferred_element_type=f32)
        values = lax.dot_general(up, value_back[rows, :], NT, preferred_element_type=f32)
        out[:both, rows] = into.astype(bf16)
        out[both:, rows] = jnp.where(half, keys, values).astype(bf16)


def lora(origin, hidden, key_back, value_back, sources):
    shape = sources[0].shape
    return pl.pallas_call(
        lora_kernel,
        out_shape=[
            jax.ShapeDtypeStruct((2 * shape[1], hidden.shape[0]), bf16),
            jax.ShapeDtypeStruct(shape, bf16),
        ],
        in_specs=[SMEM, VMEM, VMEM, VMEM] + [ANY] * 4,
        out_specs=[VMEM, VMEM],
        scratch_shapes=[pltpu.SemaphoreType.DMA((shape[0],))],
        compiler_params=params(24),
        cost_estimate=cost(2 * shape[1] * hidden.size, 2 * hidden.size + 4 * sources[0].size),
    )(origin, hidden, key_back, value_back, *sources)


def parts_kernel(hidden, key_back, value_back, t0, t1, t2, t3, part, sums):
    blocks, both, wide = part.shape
    width = hidden.shape[1]
    tokens = hidden.shape[0] // blocks
    rank = both // 2
    total = t0[...].astype(f32) + t1[...].astype(f32) + t2[...].astype(f32) + t3[...].astype(f32)
    sums[:both, :] = total[:both].astype(bf16)
    sums[both:, :] = (total[both:] * adapter_scale).astype(bf16)
    for b in range(blocks):
        rows = pl.ds(b * tokens, tokens)
        inner = sums[both:, rows]
        into = sums[:both, rows]
        down = jnp.dot(inner, hidden[rows, :], preferred_element_type=f32)
        part[b, :, :width] = down.astype(bf16)
        keys = jnp.dot(into[:rank], key_back[rows, :], preferred_element_type=f32)
        values = jnp.dot(into[rank:], value_back[rows, :], preferred_element_type=f32)
        part[b, :rank, width:] = (keys * adapter_scale).astype(bf16)
        part[b, rank:, width:] = (values * adapter_scale).astype(bf16)


def parts(hidden, key_back, value_back, pieces, blocks):
    both = pieces[0].shape[0] // 2
    shape = (blocks, both, hidden.shape[1] + key_back.shape[1])
    return pl.pallas_call(
        parts_kernel,
        out_shape=[
            jax.ShapeDtypeStruct(shape, bf16),
            jax.ShapeDtypeStruct(pieces[0].shape, bf16),
        ],
        in_specs=[VMEM] * 7,
        out_specs=[VMEM] * 2,
        compiler_params=params(24),
        cost_estimate=cost(2 * both * hidden.size, 4 * hidden.size),
    )(hidden, key_back, value_back, *pieces)


def collect_kernel(here, index, place, p0, p1, p2, p3, o0, o1, o2, o3, total):
    blocks = p0.shape[0]
    total[...] = jnp.zeros_like(total)
    for i, piece in enumerate((p0, p1, p2, p3)):
        for b in range(blocks):

            @pl.when(here[i * blocks + b] == 1)
            def _():
                slot = index[i * blocks + b]
                total[slot] = total[slot] + piece[b].astype(f32)

    for i, out in enumerate((o0, o1, o2, o3)):
        out[...] = total[pl.ds(place[i] * blocks, blocks)].astype(bf16)


def collect(here, index, place, pieces):
    shape = pieces[0].shape
    return pl.pallas_call(
        collect_kernel,
        out_shape=[jax.ShapeDtypeStruct(shape, bf16)] * 4,
        in_specs=[SMEM] * 3 + [VMEM] * 4,
        out_specs=[VMEM] * 4,
        scratch_shapes=[pltpu.VMEM((4 * shape[0],) + shape[1:], f32)],
        compiler_params=params(24),
        cost_estimate=cost(8 * pieces[0].size, 16 * pieces[0].size),
    )(here, index, place, *pieces)


def forward_kernel(place, mine, theirs, own, p0, p1, p2, p3, o0, o1, o2, o3, weights, sems):
    quarter = weights.shape[2]
    rows = mine.shape[0]
    loads = []
    for i, piece in enumerate((p0, p1, p2, p3)):
        copy = pltpu.make_async_copy(piece, weights.at[place[i]], sems.at[i])
        copy.start()
        loads.append(copy)
    for i, tokens in enumerate((mine, theirs)):
        o0[pl.ds(i * rows, rows), :] = jnp.dot(
            tokens[...], own[...], preferred_element_type=f32
        ).astype(bf16)
    for copy in loads:
        copy.wait()
    for k, out in enumerate((o1, o2, o3)):
        for i, tokens in enumerate((mine, theirs)):
            total = jnp.dot(tokens[:, :quarter], weights[0, k], preferred_element_type=f32)
            for j in range(1, 4):
                total = total + jnp.dot(
                    tokens[:, j * quarter : (j + 1) * quarter],
                    weights[j, k],
                    preferred_element_type=f32,
                )
            out[pl.ds(i * rows, rows), :] = total.astype(bf16)


def forward(place, mine, theirs, own, pieces):
    out = jax.ShapeDtypeStruct((2 * mine.shape[0], own.shape[1]), bf16)
    return pl.pallas_call(
        forward_kernel,
        out_shape=[out] * 4,
        in_specs=[SMEM] + [VMEM] * 3 + [ANY] * 4,
        out_specs=[VMEM] * 4,
        scratch_shapes=[
            pltpu.VMEM((4,) + pieces[0].shape, bf16),
            pltpu.SemaphoreType.DMA((4,)),
        ],
        compiler_params=params(40),
        cost_estimate=cost(4 * mine.size * own.shape[1] * 4, 16 * own.size),
    )(place, mine, theirs, own, *pieces)


def backward_kernel(
    place, other_place, sums, maps, b0, b1, b2, b3, own, w0, w1, w2, w3,
    other, v0, v1, v2, v3, out, weights, others, total, sems,
):
    both = maps.shape[1]
    quarter = weights.shape[2]
    blocks = maps.shape[0]
    tokens = sums.shape[1] // blocks
    loads = []
    for i, (one, two) in enumerate(((w0, v0), (w1, v1), (w2, v2), (w3, v3))):
        for k, (piece, store, at) in enumerate(
            ((one, weights, place), (two, others, other_place))
        ):
            copy = pltpu.make_async_copy(piece, store.at[at[i]], sems.at[2 * i + k])
            copy.start()
            loads.append(copy)
    for copy in loads:
        copy.wait()
    for j in range(4):
        columns = slice(j * quarter, (j + 1) * quarter)
        total[...] = lax.dot_general(
            b0[0], own[columns, :], NT, preferred_element_type=f32
        ) + lax.dot_general(b0[1], other[columns, :], NT, preferred_element_type=f32)
        for k, back in enumerate((b1, b2, b3)):
            total[...] += lax.dot_general(
                back[0], weights[j, k], NT, preferred_element_type=f32
            ) + lax.dot_general(back[1], others[j, k], NT, preferred_element_type=f32)
        for b in range(blocks):
            rows = pl.ds(b * tokens, tokens)
            out[rows, columns] = (
                total[rows, :]
                + lax.dot_general(
                    sums[both:, rows], maps[b, :, columns], TN, preferred_element_type=f32
                )
            ).astype(bf16)


def backward(place, other_place, sums, maps, backs, own, pieces, other, other_pieces):
    rows, quarter = backs[0].shape[1], pieces[0].shape[1]
    return pl.pallas_call(
        backward_kernel,
        out_shape=jax.ShapeDtypeStruct((rows, own.shape[0]), bf16),
        in_specs=[SMEM] * 2 + [VMEM] * 7 + [ANY] * 4 + [VMEM] + [ANY] * 4,
        out_specs=VMEM,
        scratch_shapes=[
            pltpu.VMEM((4,) + pieces[0].shape, bf16),
            pltpu.VMEM((4,) + pieces[0].shape, bf16),
            pltpu.VMEM((rows, quarter), f32),
            pltpu.SemaphoreType.DMA((8,)),
        ],
        compiler_params=params(48),
        cost_estimate=cost(16 * rows * own.size, 24 * own.size),
    )(place, other_place, sums, maps, *backs, own, *pieces, other, *other_pieces)


def per_device(
    hidden,
    key_weight_frozen,
    value_weight_frozen,
    adapter_down_maps,
    adapter_up_maps,
    block_adapter_index,
    segment_document_index,
    adapter_position,
    key_gradient,
    value_gradient,
):
    rows, width = hidden.shape
    kv_here = key_weight_frozen.shape[1]
    heads_here = kv_here // HEAD
    blocks = block_adapter_index.shape[0]
    block_rows = rows // blocks
    slots_here, _, rank, _ = adapter_down_maps.shape
    both = 2 * rank
    quarter = width // SIDE
    dp = lax.axis_index("dp")
    z = lax.axis_index("tensor")
    core = dp % 2
    x, y = dp // 8, (dp // 2) % 4
    line = jnp.where(core == 0, x, y)
    cross = jnp.where(core == 0, y, x)
    first = core == 0
    line_place = jnp.stack([(line - d) % SIDE for d in (0,) + SHIFTS])
    cross_place = jnp.stack([(cross - d) % SIDE for d in (0,) + SHIFTS])

    slots = jnp.take(adapter_position, block_adapter_index, axis=0)
    slots_at = [slots] + [along_cross(slots, -d) for d in SHIFTS]

    def split(slot):
        slot_x, slot_y, within = slot // 16, (slot // 4) % 4, slot % 4
        slot_line = jnp.where(first, slot_x, slot_y)
        slot_cross = jnp.where(first, slot_y, slot_x)
        local = ((within // 2 + core) % 2) * 2 + within % 2
        return slot_cross, slot_line * (2 * slots_here) + local

    maps_here = jnp.concatenate(
        [
            adapter_down_maps.reshape(slots_here, both, width),
            adapter_up_maps.reshape(slots_here, both, kv_here),
        ],
        axis=2,
    )
    maps_chip = jnp.concatenate([maps_here, to_other_core(maps_here)], axis=0)
    maps_line = [maps_chip] + [along_line(maps_chip, d) for d in SHIFTS]
    index = jnp.concatenate([split(s)[1] for s in slots_at])
    picked = pick(index, line_place, maps_line)
    maps_from = [picked[0]] + [along_cross(picked[i + 1], d) for i, d in enumerate(SHIFTS)]
    apart = (cross - split(slots)[0]) % SIDE
    origin = jnp.where(apart == 3, 2, jnp.where(apart == 2, 3, apart))

    def own_kind(start, size):
        return jnp.where(
            first,
            lax.dynamic_slice_in_dim(key_weight_frozen, start, size, 0),
            lax.dynamic_slice_in_dim(value_weight_frozen, start, size, 0),
        )

    def other_kind(start, size):
        return jnp.where(
            first,
            lax.dynamic_slice_in_dim(value_weight_frozen, start, size, 0),
            lax.dynamic_slice_in_dim(key_weight_frozen, start, size, 0),
        )

    quarters = jnp.stack(
        [
            along_z(own_kind(((z + d) % SIDE) * width + line * quarter, quarter), d)
            for d in SHIFTS
        ]
    )
    pieces = [quarters] + [along_line(quarters, d) for d in SHIFTS]
    theirs = to_other_core(hidden)
    own = own_kind(z * width, width)
    other = other_kind(z * width, width)
    partial = forward(line_place, hidden, theirs, own, pieces)
    other_pieces = [to_other_core(piece) for piece in pieces]

    cosine, sine = rope_tables(segment_document_index)
    key_back = (
        unrotate(
            key_gradient.astype(jnp.float32).reshape(rows, heads_here, HEAD), cosine, sine
        )
        .reshape(rows, kv_here)
        .astype(bf16)
    )
    back = jnp.where(
        first,
        jnp.stack([key_back, value_gradient]),
        jnp.stack([value_gradient, key_back]),
    )
    backs = [back] + [along_z(back, d) for d in SHIFTS]

    into, maps = lora(origin, hidden, key_back, value_gradient, maps_from)
    terms = [into] + [along_z(into, d) for d in SHIFTS]
    part, sums = parts(hidden, key_back, value_gradient, terms, blocks)

    hidden_gradient = backward(
        line_place, cross_place, sums, maps, backs, own, pieces, other, other_pieces
    )

    part_from = [part] + [along_cross(part, d) for d in SHIFTS]
    slots_from = [slots_at[0], slots_at[2], slots_at[1], slots_at[3]]
    found = [split(s) for s in slots_from]
    here = jnp.concatenate([(f[0] == cross).astype(jnp.int32) for f in found])
    where_to = jnp.concatenate([f[1] for f in found])
    target = jnp.stack([(line + d) % SIDE for d in (0,) + SHIFTS])
    line_sums = collect(here, where_to, target, part_from)
    arrived = [line_sums[0]] + [along_line(line_sums[i + 1], d) for i, d in enumerate(SHIFTS)]
    chip_sum = sum(a.astype(f32) for a in arrived)
    mine_sum = chip_sum[:slots_here] + to_other_core(
        chip_sum[slots_here:].astype(bf16)
    ).astype(f32)
    grad_down = mine_sum[:, :, :width].reshape(adapter_down_maps.shape)
    grad_up = mine_sum[:, :, width:].reshape(adapter_up_maps.shape)

    frozen = partial[0].astype(f32)
    for i, d in enumerate(SHIFTS):
        frozen = frozen + along_z(partial[i + 1], -d).astype(f32)
    crossed = to_other_core(frozen[rows:].astype(bf16)).astype(f32)
    adapter_input = sums[:both].reshape(2, rank, blocks, block_rows)
    added = (
        jnp.einsum(
            "jrqw,qjru->qwju",
            adapter_input,
            maps[:, :, width:].reshape(blocks, 2, rank, kv_here),
            preferred_element_type=f32,
        ).reshape(rows, 2, kv_here)
        * adapter_scale
    )
    key_pre = jnp.where(first, frozen[:rows], crossed) + added[:, 0]
    value_pre = jnp.where(first, crossed, frozen[:rows]) + added[:, 1]
    key_out = (
        rotate(key_pre.reshape(rows, heads_here, HEAD), cosine, sine)
        .reshape(rows, kv_here)
        .astype(bf16)
    )
    return key_out, value_pre.astype(bf16), hidden_gradient, grad_down, grad_up


def solution(mesh):
    return jax.shard_map(
        per_device,
        mesh=mesh,
        in_specs=(
            P("dp", "tensor"),
            P(None, "tensor"),
            P(None, "tensor"),
            P("dp", None, None, "tensor"),
            P("dp", None, None, "tensor"),
            P("dp"),
            P("dp", None),
            P(),
            P("dp", "tensor"),
            P("dp", "tensor"),
        ),
        out_specs=(
            P("dp", "tensor"),
            P("dp", "tensor"),
            P("dp", "tensor"),
            P("dp", None, None, "tensor"),
            P("dp", None, None, "tensor"),
        ),
        check_vma=False,
    )
```

```python
import math

import jax
import jax.numpy as jnp
from jax import lax
from jax.experimental import pallas as pl
from jax.experimental.pallas import tpu as pltpu
from jax.sharding import PartitionSpec as P

HEAD = 128
SIDE = 4
SHIFTS = (1, -1, 2)
SCALE = 1000
TOKEN = jax.ShapeDtypeStruct((8, HEAD), jnp.float32)

adapter_scale = 0.5
rope_theta = 500000.0
bf16 = jnp.bfloat16
f32 = jnp.float32
ANY = pl.BlockSpec(memory_space=pl.ANY)
VMEM = pl.BlockSpec(memory_space=pltpu.VMEM)
SMEM = pl.BlockSpec(memory_space=pltpu.SMEM)
NT = (((1,), (1,)), ((), ()))
TN = (((0,), (0,)), ((), ()))


def exchange(array, move):
    pairs = []
    for x in range(SIDE):
        for y in range(SIDE):
            for c in range(2):
                for z in range(SIDE):
                    x2, y2, c2, z2 = move(x, y, c, z)
                    target = (((x2 % SIDE) * SIDE + y2 % SIDE) * 2 + c2) * SIDE + z2 % SIDE
                    pairs.append((((x * SIDE + y) * 2 + c) * SIDE + z, target))
    return lax.ppermute(array, ("dp", "tensor"), pairs)


def along_z(array, shift):
    return exchange(array, lambda x, y, c, z: (x, y, c, z + shift))


def to_other_core(array):
    return exchange(array, lambda x, y, c, z: (x, y, 1 - c, z))


def along_z_apart(array, shift):
    return exchange(array, lambda x, y, c, z: (x, y, c, z + (shift if c == 0 else -shift)))


def along_line(array, shift):
    return exchange(
        array, lambda x, y, c, z: (x + shift, y, c, z) if c == 0 else (x, y + shift, c, z)
    )


def along_cross(array, shift):
    return exchange(
        array, lambda x, y, c, z: (x, y + shift, c, z) if c == 0 else (x + shift, y, c, z)
    )


def params(megabytes):
    return pltpu.CompilerParams(vmem_limit_bytes=megabytes << 20)


def cost(flops, moved):
    return pl.CostEstimate(flops=flops // SCALE, bytes_accessed=moved // SCALE, transcendentals=0)


def rope_tables(segments):
    places = jnp.arange(segments.shape[1], dtype=jnp.int32)
    earlier = jnp.concatenate([segments[:, :1] - 1, segments[:, :-1]], axis=1)
    starts = lax.cummax(jnp.where(segments != earlier, places[None, :], 0), axis=1)
    position = (places[None, :] - starts).astype(jnp.float32).reshape(-1)
    halves = jnp.arange(HEAD // 2, dtype=jnp.float32)
    inverse = jnp.exp(halves * (-2.0 * math.log(rope_theta) / HEAD))
    angles = position[:, None] * jnp.concatenate([inverse, inverse])[None, :]
    sign = jnp.where(jnp.arange(HEAD) < HEAD // 2, 1.0, -1.0)
    return jnp.stack([jnp.cos(angles), jnp.sin(angles) * sign[None, :]])


def unrotated(values, cosine, signed):
    return values * cosine + pltpu.roll(values, HEAD // 2, 1) * signed


def rotated(values, cosine, signed):
    return values * cosine - pltpu.roll(values, HEAD // 2, 1) * signed


def placed(slot, core):
    slot_x, slot_y = slot >> 4, (slot >> 2) & 3
    on_line = jnp.where(core == 0, slot_x, slot_y)
    on_cross = jnp.where(core == 0, slot_y, slot_x)
    row = ((slot & 3) + 2 * core) & 3
    return on_line, on_cross, row


def piece_from(here, there):
    apart = (here - there) & 3
    return jnp.where(apart == 3, 2, jnp.where(apart == 2, 3, apart))


def pack_kernel(count, *refs):
    out, sems = refs[-2], refs[-1]
    copies = []
    start = 0
    for i, piece in enumerate(refs[:count]):
        if piece.ndim < out.ndim:
            copies.append(pltpu.make_async_copy(piece, out.at[start], sems.at[i]))
            start += 1
        else:
            size = piece.shape[0]
            copies.append(pltpu.make_async_copy(piece, out.at[pl.ds(start, size)], sems.at[i]))
            start += size
    for copy in copies:
        copy.start()
    for copy in copies:
        copy.wait()


def pack(pieces, after=(), new_axis=False):
    if new_axis:
        shape = (len(pieces),) + pieces[0].shape
    else:
        shape = (sum(p.shape[0] for p in pieces),) + pieces[0].shape[1:]

    def kernel(*refs):
        pack_kernel(len(pieces), *refs)

    return pl.pallas_call(
        kernel,
        out_shape=jax.ShapeDtypeStruct(shape, pieces[0].dtype),
        in_specs=[ANY] * (len(pieces) + len(after)),
        out_specs=VMEM,
        scratch_shapes=[pltpu.SemaphoreType.DMA((len(pieces),))],
        compiler_params=params(16),
        cost_estimate=cost(0, 4 * math.prod(shape)),
    )(*pieces, *after)


def halves_kernel(index, at, down, up, _, mine, give, riding, sems):
    core = at[2]
    slots, both, width = down.shape
    wide = mine.shape[2] - HEAD
    lane = lax.broadcasted_iota(jnp.int32, riding.shape, 2)
    value = jnp.zeros(riding.shape, f32)
    for b in range(index.shape[0]):
        value = jnp.where(lane == b, index[b].astype(f32), value)
    riding[...] = value.astype(bf16)
    ends = [
        pltpu.make_async_copy(riding, out.at[:, :, pl.ds(wide, HEAD)], sems.at[i])
        for i, out in enumerate((mine, give))
    ]
    for copy in ends:
        copy.start()

    def halves(first, second):
        copies = [
            pltpu.make_async_copy(
                down.at[:, :, pl.ds(0, wide)], first.at[:, :, pl.ds(0, wide)], sems.at[2]
            ),
            pltpu.make_async_copy(
                down.at[:, :, pl.ds(wide, width - wide)],
                second.at[:, :, pl.ds(0, width - wide)],
                sems.at[3],
            ),
            pltpu.make_async_copy(
                up, second.at[:, :, pl.ds(width - wide, 2 * wide - width)], sems.at[4]
            ),
        ]
        for copy in copies:
            copy.start()
        for copy in copies:
            copy.wait()

    pl.when(core == 0)(lambda: halves(mine, give))
    pl.when(core == 1)(lambda: halves(give, mine))
    for copy in ends:
        copy.wait()


def split_maps(index, at, down, up, after):
    slots, both, width = down.shape
    wide = (width + up.shape[2]) // 2
    out = jax.ShapeDtypeStruct((slots, both, wide + HEAD), bf16)
    return pl.pallas_call(
        halves_kernel,
        out_shape=[out] * 2,
        in_specs=[SMEM] * 2 + [ANY] * 3,
        out_specs=[VMEM] * 2,
        scratch_shapes=[pltpu.VMEM((slots, both, HEAD), bf16), pltpu.SemaphoreType.DMA((5,))],
        compiler_params=params(16),
        cost_estimate=cost(0, 4 * down.size),
    )(index, at, down, up, after)


def lists_kernel(m0, m1, m2, m3, out, rows, sems):
    slots = m0.shape[0] // 2
    wide = m0.shape[2] - HEAD
    copies = [
        pltpu.make_async_copy(
            piece.at[k * slots, pl.ds(0, 16), pl.ds(wide, HEAD)], rows.at[2 * i + k], sems.at[2 * i + k]
        )
        for i, piece in enumerate((m0, m1, m2, m3))
        for k in range(2)
    ]
    for copy in copies:
        copy.start()
    for copy in copies:
        copy.wait()
    out[...] = rows[:, 0, :].astype(f32).astype(jnp.int32)


def riding_lists(pieces):
    return pl.pallas_call(
        lists_kernel,
        out_shape=jax.ShapeDtypeStruct((8, HEAD), jnp.int32),
        in_specs=[ANY] * 4,
        out_specs=VMEM,
        scratch_shapes=[pltpu.VMEM((8, 16, HEAD), bf16), pltpu.SemaphoreType.DMA((8,))],
        compiler_params=params(16),
        cost_estimate=cost(0, 1 << 16),
    )(*pieces)


def listed(lists, piece, b):
    return lists[2 * piece + b // 4, b % 4]


def pick_kernel(lists, positions, at, m0, m1, m2, m3, *rest):
    o1, o2, o3, sems = rest[-4:]
    line, cross, core = at[0], at[1], at[2]
    count, _, wide = o1.shape
    found = []
    for i, (row, out) in enumerate(((2, o1), (1, o2), (3, o3))):
        for b in range(count):
            on_line, on_cross, local = placed(positions[listed(lists, row, b)], core)
            piece = jnp.where(on_cross == cross, piece_from(line, on_line), SIDE)
            found.append((piece, out.at[b], sems.at[i * count + b]))
            for k, source in enumerate((m0, m1, m2, m3)):

                @pl.when(piece == k)
                def _():
                    pltpu.make_async_copy(
                        source.at[local, :, pl.ds(0, wide)], out.at[b], sems.at[i * count + b]
                    ).start()

    for piece, target, sem in found:

        @pl.when(piece < SIDE)
        def _():
            pltpu.make_async_copy(m0.at[0, :, pl.ds(0, wide)], target, sem).wait()


def pick(lists, positions, at, pieces, wide, blocks, after):
    count = 2 * blocks
    out = jax.ShapeDtypeStruct((count, pieces[0].shape[1], wide), bf16)
    return pl.pallas_call(
        pick_kernel,
        out_shape=[out] * 3,
        in_specs=[SMEM] * 3 + [ANY] * (4 + len(after)),
        out_specs=[VMEM] * 3,
        scratch_shapes=[pltpu.SemaphoreType.DMA((3 * count,))],
        compiler_params=params(60),
        cost_estimate=cost(0, 8 * pieces[0].size),
    )(lists, positions, at, *pieces, *after)


def start_block(lists, positions, at, line_pieces, cross_pieces, b, target, sem):
    line, cross, core = at[0], at[1], at[2]
    wide = cross_pieces[0].shape[2]
    on_line, on_cross, local = placed(positions[listed(lists, 0, b)], core)
    piece = piece_from(line, on_line)
    sender = piece_from(cross, on_cross)
    for k, source in enumerate(line_pieces):

        @pl.when((sender == 0) & (piece == k))
        def _():
            pltpu.make_async_copy(source.at[local, :, pl.ds(0, wide)], target, sem).start()

    for k, source in enumerate(cross_pieces):

        @pl.when(sender == k + 1)
        def _():
            pltpu.make_async_copy(source.at[b], target, sem).start()


def resolve_kernel(lists, positions, at, m0, m1, m2, m3, r1, r2, r3, mine, give, sems):
    blocks = mine.shape[0]
    targets = [give.at[b] for b in range(blocks)] + [mine.at[b] for b in range(blocks)]
    for b, target in enumerate(targets):
        start_block(lists, positions, at, (m0, m1, m2, m3), (r1, r2, r3), b, target, sems.at[b])
    for b, target in enumerate(targets):
        pltpu.make_async_copy(r1.at[0], target, sems.at[b]).wait()


def resolve(lists, positions, at, pieces, received):
    count, both, wide = received[0].shape
    out = jax.ShapeDtypeStruct((count // 2, both, wide), bf16)
    return pl.pallas_call(
        resolve_kernel,
        out_shape=[out] * 2,
        in_specs=[SMEM] * 3 + [ANY] * 7,
        out_specs=[VMEM] * 2,
        scratch_shapes=[pltpu.SemaphoreType.DMA((count,))],
        compiler_params=params(60),
        cost_estimate=cost(0, 2 * received[0].size),
    )(lists, positions, at, *pieces, *received)


def lora_kernel(at, hidden, back, mine, other, out, maps):
    core = at[2]
    blocks, both, _ = maps.shape
    wide = other.shape[2]
    width = hidden.shape[1]
    tokens = hidden.shape[0] // blocks

    @pl.when(core == 0)
    def _():
        maps[:, :, :wide] = mine[...]
        maps[:, :, wide:] = other[...]

    @pl.when(core == 1)
    def _():
        maps[:, :, :wide] = other[...]
        maps[:, :, wide:] = mine[...]

    half = lax.broadcasted_iota(jnp.int32, (both, tokens), 0) < both // 2
    for b in range(blocks):
        rows = pl.ds(b * tokens, tokens)
        down = maps[b, :, :width]
        up = maps[b, :, width:]
        into = lax.dot_general(down, hidden[rows, :], NT, preferred_element_type=f32)
        keys = lax.dot_general(up, back[0, rows, :], NT, preferred_element_type=f32)
        values = lax.dot_general(up, back[1, rows, :], NT, preferred_element_type=f32)
        out[:both, rows] = into.astype(bf16)
        out[both:, rows] = jnp.where(half, keys, values).astype(bf16)


def lora(at, hidden, back, mine, other):
    blocks, both, wide = other.shape
    return pl.pallas_call(
        lora_kernel,
        out_shape=[
            jax.ShapeDtypeStruct((2 * both, hidden.shape[0]), bf16),
            jax.ShapeDtypeStruct((blocks, both, 2 * wide), bf16),
        ],
        in_specs=[SMEM] + [VMEM] * 4,
        out_specs=[VMEM] * 2,
        compiler_params=params(24),
        cost_estimate=cost(2 * both * hidden.size, 2 * hidden.size + 4 * other.size),
    )(at, hidden, back, mine, other)


def parts_kernel(at, hidden, back, t0, t1, t2, t3, _1, _2, mine, give, sums, again, part):
    again[...] = back[...]
    core = at[2]
    blocks, both, _ = part.shape
    wide = mine.shape[2]
    width = hidden.shape[1]
    tokens = hidden.shape[0] // blocks
    rank = both // 2
    total = t0[...].astype(f32) + t1[...].astype(f32) + t2[...].astype(f32) + t3[...].astype(f32)
    sums[:both, :] = total[:both].astype(bf16)
    sums[both:, :] = (total[both:] * adapter_scale).astype(bf16)
    for b in range(blocks):
        rows = pl.ds(b * tokens, tokens)
        inner = sums[both:, rows]
        into = sums[:both, rows]
        down = jnp.dot(inner, hidden[rows, :], preferred_element_type=f32)
        part[b, :, :width] = down.astype(bf16)
        keys = jnp.dot(into[:rank], back[0, rows, :], preferred_element_type=f32)
        values = jnp.dot(into[rank:], back[1, rows, :], preferred_element_type=f32)
        part[b, :rank, width:] = (keys * adapter_scale).astype(bf16)
        part[b, rank:, width:] = (values * adapter_scale).astype(bf16)

    @pl.when(core == 0)
    def _():
        mine[...] = part[:, :, :wide]
        give[...] = part[:, :, wide:]

    @pl.when(core == 1)
    def _():
        mine[...] = part[:, :, wide:]
        give[...] = part[:, :, :wide]


def parts(at, hidden, back, pieces, blocks, after):
    both = pieces[0].shape[0] // 2
    wide = (hidden.shape[1] + back.shape[2]) // 2
    return pl.pallas_call(
        parts_kernel,
        out_shape=[
            jax.ShapeDtypeStruct((blocks, both, wide), bf16),
            jax.ShapeDtypeStruct((blocks, both, wide), bf16),
            jax.ShapeDtypeStruct(pieces[0].shape, bf16),
            jax.ShapeDtypeStruct(back.shape, bf16),
        ],
        in_specs=[SMEM] + [VMEM] * 6 + [ANY] * 2,
        out_specs=[VMEM] * 4,
        scratch_shapes=[pltpu.VMEM((blocks, both, 2 * wide), bf16)],
        compiler_params=params(24),
        cost_estimate=cost(2 * both * hidden.size, 4 * hidden.size),
    )(at, hidden, back, *pieces, *after)


def collect_kernel(lists, positions, at, p0, p1, p2, p3, *rest):
    o0, o1, o2, o3, total = rest[-5:]
    line, cross, core = at[0], at[1], at[2]
    slots = o0.shape[0]
    total[...] = jnp.zeros_like(total)
    for i, piece in enumerate((p0, p1, p2, p3)):
        for b in range(piece.shape[0]):
            on_line, on_cross, local = placed(positions[listed(lists, i, b)], core)

            @pl.when(on_cross == cross)
            def _():
                slot = on_line * slots + local
                total[slot] = total[slot] + piece[b].astype(f32)

    for shift, out in zip((0,) + SHIFTS, (o0, o1, o2, o3)):
        target = (line + shift + SIDE) % SIDE
        out[...] = total[pl.ds(target * slots, slots)].astype(bf16)


def collect(lists, positions, at, pieces, slots, after):
    _, both, wide = pieces[0].shape
    return pl.pallas_call(
        collect_kernel,
        out_shape=[jax.ShapeDtypeStruct((slots, both, wide), bf16)] * 4,
        in_specs=[SMEM] * 3 + [VMEM] * 4 + [ANY] * len(after),
        out_specs=[VMEM] * 4,
        scratch_shapes=[pltpu.VMEM((4 * slots, both, wide), f32)],
        compiler_params=params(60),
        cost_estimate=cost(8 * pieces[0].size, 16 * pieces[0].size),
    )(lists, positions, at, *pieces, *after)


def turn_kernel(tables, key_grad, value_grad, back):
    for h in range(key_grad.shape[1] // HEAD):
        lanes = slice(h * HEAD, (h + 1) * HEAD)
        back[0, :, lanes] = unrotated(
            key_grad[:, lanes].astype(f32), tables[0], tables[1]
        ).astype(bf16)
    back[1] = value_grad[...]


def turn(tables, key_grad, value_grad):
    return pl.pallas_call(
        turn_kernel,
        out_shape=jax.ShapeDtypeStruct((2,) + key_grad.shape, bf16),
        in_specs=[VMEM] * 3,
        out_specs=VMEM,
        compiler_params=params(16),
        cost_estimate=cost(0, 10 * key_grad.size),
    )(tables, key_grad, value_grad)


def send_kernel(at, keys, values, near, far, sems):
    core, z = at[2], at[3]
    width = far.shape[0]

    def copies(mine, theirs, shift):
        rows = pl.ds(pl.multiple_of(((z + shift + SIDE) % SIDE) * width, 256), width)
        across = pl.ds(pl.multiple_of(((z + 2) % SIDE) * width, 256), width)
        found = [
            pltpu.make_async_copy(mine.at[rows], near.at[0], sems.at[0]),
            pltpu.make_async_copy(theirs.at[rows], near.at[1], sems.at[1]),
            pltpu.make_async_copy(mine.at[across], far, sems.at[2]),
        ]
        for copy in found:
            copy.start()
        for copy in found:
            copy.wait()

    pl.when(core == 0)(lambda: copies(keys, values, 1))
    pl.when(core == 1)(lambda: copies(values, keys, -1))


def to_send(at, keys, values):
    rows, kv = keys.shape[0] // SIDE, keys.shape[1]
    return pl.pallas_call(
        send_kernel,
        out_shape=[
            jax.ShapeDtypeStruct((2, rows, kv), bf16),
            jax.ShapeDtypeStruct((rows, kv), bf16),
        ],
        in_specs=[SMEM] + [ANY] * 2,
        out_specs=[VMEM] * 2,
        scratch_shapes=[pltpu.SemaphoreType.DMA((3,))],
        compiler_params=params(60),
        cost_estimate=cost(0, 12 * rows * kv),
    )(at, keys, values)


def weight_sources(at, keys, values, near, near_theirs, far, far_theirs):
    core = at[2]
    found = []
    for kind in range(2):
        own = ((keys, (core + kind) % 2 == 0), (values, (core + kind) % 2 == 1))
        found.append(own)
        for piece in (near.at[kind], near_theirs.at[1 - kind], (far, far_theirs)[kind]):
            found.append(((piece, None),))
    return found


def start_weights(sources, own_rows, rows, target, sem):
    for source, condition in sources:
        if condition is None:
            pltpu.make_async_copy(source.at[rows], target, sem).start()
        else:

            @pl.when(condition)
            def _():
                pltpu.make_async_copy(source.at[own_rows], target, sem).start()


def forward_kernel(
    at, hidden, keys, values, near, near_theirs, far, far_theirs, _, o0, o1, o2, o3, done, weights, sems
):
    width = weights.shape[1]
    sources = weight_sources(at, keys, values, near, near_theirs, far, far_theirs)
    own_rows = pl.ds(pl.multiple_of(at[3] * width, 256), width)
    order = [4 * kind + k for k in range(4) for kind in range(2)]

    def start(step):
        i = order[step]
        start_weights(sources[i], own_rows, pl.ds(0, width), weights.at[i], sems.at[i])

    for step in range(3):
        start(step)
    done[...] = jnp.zeros_like(done)
    for step, i in enumerate(order):
        if step + 3 < len(order):
            start(step + 3)
        pltpu.make_async_copy(far, weights.at[i], sems.at[i]).wait()
        (o0, o1, o2, o3)[i % 4][i // 4] = jnp.dot(
            hidden[...], weights[i], preferred_element_type=f32
        ).astype(bf16)


def forward(at, hidden, keys, values, pieces, after):
    rows, width = hidden.shape
    kv = keys.shape[1]
    out = jax.ShapeDtypeStruct((2, rows, kv), bf16)
    return pl.pallas_call(
        forward_kernel,
        out_shape=[out] * 4 + [TOKEN],
        in_specs=[SMEM, VMEM] + [ANY] * 7,
        out_specs=[VMEM] * 5,
        scratch_shapes=[pltpu.VMEM((8, width, kv), bf16), pltpu.SemaphoreType.DMA((8,))],
        compiler_params=params(40),
        cost_estimate=cost(SCALE * 32 * hidden.size * kv, SCALE * 32 * width * kv),
    )(at, hidden, keys, values, *pieces, after)


def backward_kernel(
    at, b0, b1, b2, b3, keys, values, near, near_theirs, far, far_theirs, sums, maps, *rest
):
    out, done, weights, back, sems = rest[-5:]
    core, z = at[2], at[3]
    kv = b0.shape[2]
    width = weights.shape[1]
    quarter = width // SIDE
    blocks, both, _ = maps.shape
    sources = weight_sources(at, keys, values, near, near_theirs, far, far_theirs)

    def load(j):
        rows = pl.ds(j * quarter, quarter)
        own_rows = pl.ds(pl.multiple_of(z * width + j * quarter, 256), quarter)
        for i in range(8):
            start_weights(sources[i], own_rows, rows, weights.at[i, rows], sems.at[8 * j + i])

    load(0)
    load(1)
    done[...] = jnp.zeros_like(done)
    for kind in range(2):
        for k, part in enumerate((b0, b1, b2, b3)):
            start = (4 * kind + k) * kv
            back[:, start : start + kv] = part[(core + kind) % 2]
    for j in range(SIDE):
        rows = pl.ds(j * quarter, quarter)
        if j + 2 < SIDE:
            load(j + 2)
        for i in range(8):
            pltpu.make_async_copy(far.at[rows], weights.at[i, rows], sems.at[8 * j + i]).wait()
        columns = slice(j * quarter, (j + 1) * quarter)
        wide = jnp.concatenate([weights[i, columns, :] for i in range(8)], axis=1)
        total = lax.dot_general(back[...], wide, NT, preferred_element_type=f32)
        tokens = total.shape[0] // blocks
        for b in range(blocks):
            block = slice(b * tokens, (b + 1) * tokens)
            out[block, columns] = (
                total[block, :]
                + lax.dot_general(
                    sums[both:, block], maps[b, :, columns], TN, preferred_element_type=f32
                )
            ).astype(bf16)


def backward(at, backs, keys, values, pieces, sums, maps, after):
    _, rows, kv = backs[0].shape
    width = keys.shape[0] // SIDE
    return pl.pallas_call(
        backward_kernel,
        out_shape=[jax.ShapeDtypeStruct((rows, width), bf16), TOKEN],
        in_specs=[SMEM] + [VMEM] * 4 + [ANY] * 6 + [VMEM] * 2 + [ANY] * len(after),
        out_specs=[VMEM] * 2,
        scratch_shapes=[
            pltpu.VMEM((8, width, kv), bf16),
            pltpu.VMEM((rows, 8 * kv), bf16),
            pltpu.SemaphoreType.DMA((32,)),
        ],
        compiler_params=params(60),
        cost_estimate=cost(SCALE * 48 * rows * width * kv, SCALE * 32 * width * kv),
    )(at, *backs, keys, values, *pieces, sums, maps, *after)


def finish_kernel(at, sums, maps, tables, t0, t1, t2, t3, _, key_out, value_out):
    core = at[2]
    blocks, both, wide = maps.shape
    rank = both // 2
    rows, kv = key_out.shape
    tokens = rows // blocks
    for b in range(blocks):
        block = slice(b * tokens, (b + 1) * tokens)
        for kind, out in enumerate((key_out, value_out)):
            first = kind * rank
            total = sum(t[(core + kind) % 2, block].astype(f32) for t in (t0, t1, t2, t3))
            total = total + adapter_scale * lax.dot_general(
                sums[first : first + rank, block],
                maps[b, first : first + rank, wide - kv :],
                TN,
                preferred_element_type=f32,
            )
            if kind == 1:
                out[block, :] = total.astype(bf16)
            else:
                for h in range(kv // HEAD):
                    lanes = slice(h * HEAD, (h + 1) * HEAD)
                    out[block, lanes] = rotated(
                        total[:, lanes], tables[0, block, :], tables[1, block, :]
                    ).astype(bf16)


def finish(at, sums, maps, tables, terms, after):
    _, rows, kv = terms[0].shape
    return pl.pallas_call(
        finish_kernel,
        out_shape=[jax.ShapeDtypeStruct((rows, kv), bf16)] * 2,
        in_specs=[SMEM] + [VMEM] * 7 + [ANY],
        out_specs=[VMEM] * 2,
        compiler_params=params(24),
        cost_estimate=cost(0, 16 * terms[0].size),
    )(at, sums, maps, tables, *terms, after)


def give_kernel(a0, a1, a2, a3, *rest):
    out = rest[-1]
    n = out.shape[0]
    out[...] = sum(a[n:].astype(f32) for a in (a0, a1, a2, a3))


def sums_kernel(at, a0, a1, a2, a3, crossed, down, up):
    core = at[2]
    n, _, width = down.shape
    wide = crossed.shape[2]
    mine = sum(a[:n].astype(f32) for a in (a0, a1, a2, a3))

    def store(first, second):
        down[:, :, :wide] = first
        down[:, :, wide:] = second[:, :, : width - wide]
        up[...] = second[:, :, width - wide :]

    pl.when(core == 0)(lambda: store(mine, crossed[...]))
    pl.when(core == 1)(lambda: store(crossed[...], mine))


def gather_sums(at, arrived, slots_here, width, after):
    _, both, wide = arrived[0].shape
    give = pl.pallas_call(
        give_kernel,
        out_shape=jax.ShapeDtypeStruct((slots_here, both, wide), f32),
        in_specs=[VMEM] * 4 + [ANY] * len(after),
        out_specs=VMEM,
        compiler_params=params(16),
        cost_estimate=cost(0, 8 * arrived[0].size),
    )(*arrived, *after)
    return pl.pallas_call(
        sums_kernel,
        out_shape=[
            jax.ShapeDtypeStruct((slots_here, both, width), f32),
            jax.ShapeDtypeStruct((slots_here, both, 2 * wide - width), f32),
        ],
        in_specs=[SMEM] + [VMEM] * 5,
        out_specs=[VMEM] * 2,
        compiler_params=params(16),
        cost_estimate=cost(0, 8 * arrived[0].size),
    )(at, *arrived, to_other_core(give))


def per_device(
    hidden,
    key_weight_frozen,
    value_weight_frozen,
    adapter_down_maps,
    adapter_up_maps,
    block_adapter_index,
    segment_document_index,
    adapter_position,
    key_gradient,
    value_gradient,
):
    width = hidden.shape[1]
    kv_here = key_weight_frozen.shape[1]
    blocks = block_adapter_index.shape[0]
    slots_here, _, rank, _ = adapter_down_maps.shape
    both = 2 * rank
    wide = width + kv_here
    quarter = width // SIDE
    dp = lax.axis_index("dp")
    z = lax.axis_index("tensor")
    core = dp % 2
    x, y = dp // 8, (dp // 2) % 4
    first = core == 0
    line = jnp.where(first, x, y)
    cross = jnp.where(first, y, x)
    at = jnp.stack([line, cross, core, z])

    half = wide // 2
    sent_near, sent_far = to_send(at, key_weight_frozen, value_weight_frozen)
    mine_half, give_half = split_maps(
        block_adapter_index,
        at,
        adapter_down_maps.reshape(slots_here, both, width),
        adapter_up_maps.reshape(slots_here, both, kv_here),
        sent_near,
    )
    maps_chip = pack([mine_half, to_other_core(give_half)])
    maps_line = [maps_chip] + [along_line(maps_chip, d) for d in SHIFTS]
    lists_here = riding_lists(maps_line)
    lists = to_other_core(lists_here)
    sent_far, _ = lax.optimization_barrier((sent_far, lists_here))
    segments, _ = lax.optimization_barrier((segment_document_index, maps_chip))
    tables = rope_tables(segments)
    back = turn(tables, key_gradient, value_gradient)
    picked = pick(lists, adapter_position, at, maps_line, half, blocks, (back,))
    received = [along_cross(p, d) for p, d in zip(picked, SHIFTS)]

    near = along_z_apart(sent_near, 1)
    far = along_z(sent_far, 2)
    mine_maps, give_maps = resolve(lists, adapter_position, at, maps_line, received)
    into, maps = lora(at, hidden, back, mine_maps, to_other_core(give_maps))
    near, far, _ = lax.optimization_barrier((near, far, into))
    pieces = [near, to_other_core(near), far, to_other_core(far)]
    terms = [into] + [along_z(into, d) for d in SHIFTS]
    part_mine, part_give, sums, back = parts(
        at, hidden, back, terms, blocks, (pieces[1], pieces[3])
    )
    part = pack([to_other_core(part_give), part_mine])
    *partial, forward_done = forward(
        at, hidden, key_weight_frozen, value_weight_frozen, pieces, part
    )

    part_from = [part] + [along_cross(part, d) for d in SHIFTS]
    back_later, _ = lax.optimization_barrier((back, forward_done))
    backs = [back, along_z_apart(back, 1), along_z_apart(back, -1), along_z(back_later, 2)]
    line_sums = collect(
        lists, adapter_position, at, part_from, 2 * slots_here, [forward_done] + backs[1:3]
    )
    arrived = [line_sums[0]] + [along_line(s, d) for s, d in zip(line_sums[1:], SHIFTS)]
    key_terms = [
        partial[0],
        along_z_apart(partial[1], -1),
        along_z_apart(partial[2], 1),
        along_z(partial[3], 2),
    ]
    hidden_gradient, backward_done = backward(
        at, backs, key_weight_frozen, value_weight_frozen, pieces, sums, maps, line_sums[:1]
    )
    grad_down, grad_up = gather_sums(at, arrived, slots_here, width, (backward_done,))
    key_out, value_out = finish(at, sums, maps, tables, key_terms, backward_done)
    return (
        key_out,
        value_out,
        hidden_gradient,
        grad_down.reshape(adapter_down_maps.shape),
        grad_up.reshape(adapter_up_maps.shape),
    )


def solution(mesh):
    return jax.shard_map(
        per_device,
        mesh=mesh,
        in_specs=(
            P("dp", "tensor"),
            P(None, "tensor"),
            P(None, "tensor"),
            P("dp", None, None, "tensor"),
            P("dp", None, None, "tensor"),
            P("dp"),
            P("dp", None),
            P(),
            P("dp", "tensor"),
            P("dp", "tensor"),
        ),
        out_specs=(
            P("dp", "tensor"),
            P("dp", "tensor"),
            P("dp", "tensor"),
            P("dp", None, None, "tensor"),
            P("dp", None, None, "tensor"),
        ),
        check_vma=False,
    )
```

```python
import math

import jax
import jax.numpy as jnp
from jax import lax
from jax.experimental import pallas as pl
from jax.experimental.pallas import tpu as pltpu
from jax.sharding import PartitionSpec as P

HEAD = 128
SIDE = 4
SHIFTS = (1, -1, 2)
SCALE = 1000
TOKEN = jax.ShapeDtypeStruct((8, HEAD), jnp.float32)

adapter_scale = 0.5
rope_theta = 500000.0
bf16 = jnp.bfloat16
f32 = jnp.float32
ANY = pl.BlockSpec(memory_space=pl.ANY)
VMEM = pl.BlockSpec(memory_space=pltpu.VMEM)
SMEM = pl.BlockSpec(memory_space=pltpu.SMEM)
NT = (((1,), (1,)), ((), ()))
TN = (((0,), (0,)), ((), ()))


def exchange(array, move):
    pairs = []
    for x in range(SIDE):
        for y in range(SIDE):
            for c in range(2):
                for z in range(SIDE):
                    x2, y2, c2, z2 = move(x, y, c, z)
                    target = (((x2 % SIDE) * SIDE + y2 % SIDE) * 2 + c2) * SIDE + z2 % SIDE
                    pairs.append((((x * SIDE + y) * 2 + c) * SIDE + z, target))
    return lax.ppermute(array, ("dp", "tensor"), pairs)


def along_z(array, shift):
    return exchange(array, lambda x, y, c, z: (x, y, c, z + shift))


def to_other_core(array):
    return exchange(array, lambda x, y, c, z: (x, y, 1 - c, z))


def along_z_apart(array, shift):
    return exchange(array, lambda x, y, c, z: (x, y, c, z + (shift if c == 0 else -shift)))


def along_line(array, shift):
    return exchange(
        array, lambda x, y, c, z: (x + shift, y, c, z) if c == 0 else (x, y + shift, c, z)
    )


def along_cross(array, shift):
    return exchange(
        array, lambda x, y, c, z: (x, y + shift, c, z) if c == 0 else (x + shift, y, c, z)
    )


def params(megabytes):
    return pltpu.CompilerParams(vmem_limit_bytes=megabytes << 20)


def cost(flops, moved):
    return pl.CostEstimate(flops=flops // SCALE, bytes_accessed=moved // SCALE, transcendentals=0)


def rope_tables(segments):
    places = jnp.arange(segments.shape[1], dtype=jnp.int32)
    earlier = jnp.concatenate([segments[:, :1] - 1, segments[:, :-1]], axis=1)
    starts = lax.cummax(jnp.where(segments != earlier, places[None, :], 0), axis=1)
    position = (places[None, :] - starts).astype(jnp.float32).reshape(-1)
    halves = jnp.arange(HEAD // 2, dtype=jnp.float32)
    inverse = jnp.exp(halves * (-2.0 * math.log(rope_theta) / HEAD))
    angles = position[:, None] * jnp.concatenate([inverse, inverse])[None, :]
    sign = jnp.where(jnp.arange(HEAD) < HEAD // 2, 1.0, -1.0)
    return jnp.stack([jnp.cos(angles), jnp.sin(angles) * sign[None, :]])


def unrotated(values, cosine, signed):
    return values * cosine + pltpu.roll(values, HEAD // 2, 1) * signed


def rotated(values, cosine, signed):
    return values * cosine - pltpu.roll(values, HEAD // 2, 1) * signed


def placed(slot, core):
    slot_x, slot_y = slot >> 4, (slot >> 2) & 3
    on_line = jnp.where(core == 0, slot_x, slot_y)
    on_cross = jnp.where(core == 0, slot_y, slot_x)
    row = ((slot & 3) + 2 * core) & 3
    return on_line, on_cross, row


def piece_from(here, there):
    apart = (here - there) & 3
    return jnp.where(apart == 3, 2, jnp.where(apart == 2, 3, apart))


def pack_kernel(count, *refs):
    out, sems = refs[-2], refs[-1]
    copies = []
    start = 0
    for i, piece in enumerate(refs[:count]):
        if piece.ndim < out.ndim:
            copies.append(pltpu.make_async_copy(piece, out.at[start], sems.at[i]))
            start += 1
        else:
            size = piece.shape[0]
            copies.append(pltpu.make_async_copy(piece, out.at[pl.ds(start, size)], sems.at[i]))
            start += size
    for copy in copies:
        copy.start()
    for copy in copies:
        copy.wait()


def pack(pieces, after=(), new_axis=False):
    if new_axis:
        shape = (len(pieces),) + pieces[0].shape
    else:
        shape = (sum(p.shape[0] for p in pieces),) + pieces[0].shape[1:]

    def kernel(*refs):
        pack_kernel(len(pieces), *refs)

    return pl.pallas_call(
        kernel,
        out_shape=jax.ShapeDtypeStruct(shape, pieces[0].dtype),
        in_specs=[ANY] * (len(pieces) + len(after)),
        out_specs=VMEM,
        scratch_shapes=[pltpu.SemaphoreType.DMA((len(pieces),))],
        compiler_params=params(16),
        cost_estimate=cost(0, 4 * math.prod(shape)),
    )(*pieces, *after)


def halves_kernel(index, at, down, up, _, mine, give, riding, sems):
    core = at[2]
    slots, both, width = down.shape
    wide = mine.shape[2] - HEAD
    lane = lax.broadcasted_iota(jnp.int32, riding.shape, 2)
    value = jnp.zeros(riding.shape, f32)
    for b in range(index.shape[0]):
        value = jnp.where(lane == b, index[b].astype(f32), value)
    riding[...] = value.astype(bf16)
    ends = [
        pltpu.make_async_copy(riding, out.at[:, :, pl.ds(wide, HEAD)], sems.at[i])
        for i, out in enumerate((mine, give))
    ]
    for copy in ends:
        copy.start()

    def halves(first, second):
        copies = [
            pltpu.make_async_copy(
                down.at[:, :, pl.ds(0, wide)], first.at[:, :, pl.ds(0, wide)], sems.at[2]
            ),
            pltpu.make_async_copy(
                down.at[:, :, pl.ds(wide, width - wide)],
                second.at[:, :, pl.ds(0, width - wide)],
                sems.at[3],
            ),
            pltpu.make_async_copy(
                up, second.at[:, :, pl.ds(width - wide, 2 * wide - width)], sems.at[4]
            ),
        ]
        for copy in copies:
            copy.start()
        for copy in copies:
            copy.wait()

    pl.when(core == 0)(lambda: halves(mine, give))
    pl.when(core == 1)(lambda: halves(give, mine))
    for copy in ends:
        copy.wait()


def split_maps(index, at, down, up, after):
    slots, both, width = down.shape
    wide = (width + up.shape[2]) // 2
    out = jax.ShapeDtypeStruct((slots, both, wide + HEAD), bf16)
    return pl.pallas_call(
        halves_kernel,
        out_shape=[out] * 2,
        in_specs=[SMEM] * 2 + [ANY] * 3,
        out_specs=[VMEM] * 2,
        scratch_shapes=[pltpu.VMEM((slots, both, HEAD), bf16), pltpu.SemaphoreType.DMA((5,))],
        compiler_params=params(16),
        cost_estimate=cost(0, 4 * down.size),
    )(index, at, down, up, after)


def lists_kernel(m0, m1, m2, m3, out, rows, sems):
    slots = m0.shape[0] // 2
    wide = m0.shape[2] - HEAD
    copies = [
        pltpu.make_async_copy(
            piece.at[k * slots, pl.ds(0, 16), pl.ds(wide, HEAD)], rows.at[2 * i + k], sems.at[2 * i + k]
        )
        for i, piece in enumerate((m0, m1, m2, m3))
        for k in range(2)
    ]
    for copy in copies:
        copy.start()
    for copy in copies:
        copy.wait()
    out[...] = rows[:, 0, :].astype(f32).astype(jnp.int32)


def riding_lists(pieces):
    return pl.pallas_call(
        lists_kernel,
        out_shape=jax.ShapeDtypeStruct((8, HEAD), jnp.int32),
        in_specs=[ANY] * 4,
        out_specs=VMEM,
        scratch_shapes=[pltpu.VMEM((8, 16, HEAD), bf16), pltpu.SemaphoreType.DMA((8,))],
        compiler_params=params(16),
        cost_estimate=cost(0, 1 << 16),
    )(*pieces)


def listed(lists, piece, b):
    return lists[2 * piece + b // 4, b % 4]


def pick_kernel(lists, positions, at, m0, m1, m2, m3, *rest):
    o1, o2, o3, sems = rest[-4:]
    line, cross, core = at[0], at[1], at[2]
    count, _, wide = o1.shape
    found = []
    for i, (row, out) in enumerate(((2, o1), (1, o2), (3, o3))):
        for b in range(count):
            on_line, on_cross, local = placed(positions[listed(lists, row, b)], core)
            piece = jnp.where(on_cross == cross, piece_from(line, on_line), SIDE)
            found.append((piece, out.at[b], sems.at[i * count + b]))
            for k, source in enumerate((m0, m1, m2, m3)):

                @pl.when(piece == k)
                def _():
                    pltpu.make_async_copy(
                        source.at[local, :, pl.ds(0, wide)], out.at[b], sems.at[i * count + b]
                    ).start()

    for piece, target, sem in found:

        @pl.when(piece < SIDE)
        def _():
            pltpu.make_async_copy(m0.at[0, :, pl.ds(0, wide)], target, sem).wait()


def pick(lists, positions, at, pieces, wide, blocks, after):
    count = 2 * blocks
    out = jax.ShapeDtypeStruct((count, pieces[0].shape[1], wide), bf16)
    return pl.pallas_call(
        pick_kernel,
        out_shape=[out] * 3,
        in_specs=[SMEM] * 3 + [ANY] * (4 + len(after)),
        out_specs=[VMEM] * 3,
        scratch_shapes=[pltpu.SemaphoreType.DMA((3 * count,))],
        compiler_params=params(60),
        cost_estimate=cost(0, 8 * pieces[0].size),
    )(lists, positions, at, *pieces, *after)


def start_block(lists, positions, at, line_pieces, cross_pieces, b, target, sem):
    line, cross, core = at[0], at[1], at[2]
    wide = cross_pieces[0].shape[2]
    on_line, on_cross, local = placed(positions[listed(lists, 0, b)], core)
    piece = piece_from(line, on_line)
    sender = piece_from(cross, on_cross)
    for k, source in enumerate(line_pieces):

        @pl.when((sender == 0) & (piece == k))
        def _():
            pltpu.make_async_copy(source.at[local, :, pl.ds(0, wide)], target, sem).start()

    for k, source in enumerate(cross_pieces):

        @pl.when(sender == k + 1)
        def _():
            pltpu.make_async_copy(source.at[b], target, sem).start()


def resolve_kernel(lists, positions, at, m0, m1, m2, m3, r1, r2, r3, mine, give, sems):
    blocks = mine.shape[0]
    targets = [give.at[b] for b in range(blocks)] + [mine.at[b] for b in range(blocks)]
    for b, target in enumerate(targets):
        start_block(lists, positions, at, (m0, m1, m2, m3), (r1, r2, r3), b, target, sems.at[b])
    for b, target in enumerate(targets):
        pltpu.make_async_copy(r1.at[0], target, sems.at[b]).wait()


def resolve(lists, positions, at, pieces, received):
    count, both, wide = received[0].shape
    out = jax.ShapeDtypeStruct((count // 2, both, wide), bf16)
    return pl.pallas_call(
        resolve_kernel,
        out_shape=[out] * 2,
        in_specs=[SMEM] * 3 + [ANY] * 7,
        out_specs=[VMEM] * 2,
        scratch_shapes=[pltpu.SemaphoreType.DMA((count,))],
        compiler_params=params(60),
        cost_estimate=cost(0, 2 * received[0].size),
    )(lists, positions, at, *pieces, *received)


def lora_kernel(at, hidden, back, mine, other, out, maps):
    core = at[2]
    blocks, both, _ = maps.shape
    wide = other.shape[2]
    width = hidden.shape[1]
    tokens = hidden.shape[0] // blocks

    @pl.when(core == 0)
    def _():
        maps[:, :, :wide] = mine[...]
        maps[:, :, wide:] = other[...]

    @pl.when(core == 1)
    def _():
        maps[:, :, :wide] = other[...]
        maps[:, :, wide:] = mine[...]

    half = lax.broadcasted_iota(jnp.int32, (both, tokens), 0) < both // 2
    for b in range(blocks):
        rows = pl.ds(b * tokens, tokens)
        down = maps[b, :, :width]
        up = maps[b, :, width:]
        into = lax.dot_general(down, hidden[rows, :], NT, preferred_element_type=f32)
        keys = lax.dot_general(up, back[0, rows, :], NT, preferred_element_type=f32)
        values = lax.dot_general(up, back[1, rows, :], NT, preferred_element_type=f32)
        out[:both, rows] = into.astype(bf16)
        out[both:, rows] = jnp.where(half, keys, values).astype(bf16)


def lora(at, hidden, back, mine, other):
    blocks, both, wide = other.shape
    return pl.pallas_call(
        lora_kernel,
        out_shape=[
            jax.ShapeDtypeStruct((2 * both, hidden.shape[0]), bf16),
            jax.ShapeDtypeStruct((blocks, both, 2 * wide), bf16),
        ],
        in_specs=[SMEM] + [VMEM] * 4,
        out_specs=[VMEM] * 2,
        compiler_params=params(24),
        cost_estimate=cost(2 * both * hidden.size, 2 * hidden.size + 4 * other.size),
    )(at, hidden, back, mine, other)


def parts_kernel(at, hidden, back, t0, t1, t2, t3, _1, _2, mine, give, sums, again, part):
    again[...] = back[...]
    core = at[2]
    blocks, both, _ = part.shape
    wide = mine.shape[2]
    width = hidden.shape[1]
    tokens = hidden.shape[0] // blocks
    rank = both // 2
    total = t0[...].astype(f32) + t1[...].astype(f32) + t2[...].astype(f32) + t3[...].astype(f32)
    sums[:both, :] = total[:both].astype(bf16)
    sums[both:, :] = (total[both:] * adapter_scale).astype(bf16)
    for b in range(blocks):
        rows = pl.ds(b * tokens, tokens)
        inner = sums[both:, rows]
        into = sums[:both, rows]
        down = jnp.dot(inner, hidden[rows, :], preferred_element_type=f32)
        part[b, :, :width] = down.astype(bf16)
        keys = jnp.dot(into[:rank], back[0, rows, :], preferred_element_type=f32)
        values = jnp.dot(into[rank:], back[1, rows, :], preferred_element_type=f32)
        part[b, :rank, width:] = (keys * adapter_scale).astype(bf16)
        part[b, rank:, width:] = (values * adapter_scale).astype(bf16)

    @pl.when(core == 0)
    def _():
        mine[...] = part[:, :, :wide]
        give[...] = part[:, :, wide:]

    @pl.when(core == 1)
    def _():
        mine[...] = part[:, :, wide:]
        give[...] = part[:, :, :wide]


def parts(at, hidden, back, pieces, blocks, after):
    both = pieces[0].shape[0] // 2
    wide = (hidden.shape[1] + back.shape[2]) // 2
    return pl.pallas_call(
        parts_kernel,
        out_shape=[
            jax.ShapeDtypeStruct((blocks, both, wide), bf16),
            jax.ShapeDtypeStruct((blocks, both, wide), bf16),
            jax.ShapeDtypeStruct(pieces[0].shape, bf16),
            jax.ShapeDtypeStruct(back.shape, bf16),
        ],
        in_specs=[SMEM] + [VMEM] * 6 + [ANY] * 2,
        out_specs=[VMEM] * 4,
        scratch_shapes=[pltpu.VMEM((blocks, both, 2 * wide), bf16)],
        compiler_params=params(24),
        cost_estimate=cost(2 * both * hidden.size, 4 * hidden.size),
    )(at, hidden, back, *pieces, *after)


def collect_kernel(lists, positions, at, p0, p1, p2, p3, *rest):
    o0, o1, o2, o3, total, held, sems = rest[-7:]
    line, cross, core = at[0], at[1], at[2]
    slots = o0.shape[0]
    found = []
    for i, piece in enumerate((p0, p1, p2, p3)):
        for b in range(piece.shape[0]):
            on_line, on_cross, local = placed(positions[lists[2 * i + b // 4, b % 4]], core)
            n = len(found)
            found.append((on_cross == cross, on_line * slots + local))

            @pl.when(on_cross == cross)
            def _():
                pltpu.make_async_copy(piece.at[b], held.at[n], sems.at[n]).start()

    total[...] = jnp.zeros_like(total)
    for n, (here, slot) in enumerate(found):

        @pl.when(here)
        def _():
            pltpu.make_async_copy(p0.at[0], held.at[n], sems.at[n]).wait()
            total[slot] = total[slot] + held[n].astype(f32)

    for shift, out in zip((0,) + SHIFTS, (o0, o1, o2, o3)):
        target = (line + shift + SIDE) % SIDE
        out[...] = total[pl.ds(target * slots, slots)].astype(bf16)


def collect(lists, positions, at, pieces, slots, after):
    count, both, wide = pieces[0].shape
    return pl.pallas_call(
        collect_kernel,
        out_shape=[jax.ShapeDtypeStruct((slots, both, wide), bf16)] * 4,
        in_specs=[SMEM] * 3 + [ANY] * (4 + len(after)),
        out_specs=[VMEM] * 4,
        scratch_shapes=[
            pltpu.VMEM((4 * slots, both, wide), f32),
            pltpu.VMEM((4 * count, both, wide), bf16),
            pltpu.SemaphoreType.DMA((4 * count,)),
        ],
        compiler_params=params(60),
        cost_estimate=cost(8 * pieces[0].size, 16 * pieces[0].size),
    )(lists, positions, at, *pieces, *after)


def turn_kernel(tables, key_grad, value_grad, back):
    for h in range(key_grad.shape[1] // HEAD):
        lanes = slice(h * HEAD, (h + 1) * HEAD)
        back[0, :, lanes] = unrotated(
            key_grad[:, lanes].astype(f32), tables[0], tables[1]
        ).astype(bf16)
    back[1] = value_grad[...]


def turn(tables, key_grad, value_grad):
    return pl.pallas_call(
        turn_kernel,
        out_shape=jax.ShapeDtypeStruct((2,) + key_grad.shape, bf16),
        in_specs=[VMEM] * 3,
        out_specs=VMEM,
        compiler_params=params(16),
        cost_estimate=cost(0, 10 * key_grad.size),
    )(tables, key_grad, value_grad)


def send_kernel(at, keys, values, near, far, done, sems):
    done[...] = jnp.zeros_like(done)
    core, z = at[2], at[3]
    width = far.shape[0]

    def copies(mine, theirs, shift):
        rows = pl.ds(pl.multiple_of(((z + shift + SIDE) % SIDE) * width, 256), width)
        across = pl.ds(pl.multiple_of(((z + 2) % SIDE) * width, 256), width)
        found = [
            pltpu.make_async_copy(mine.at[rows], near.at[0], sems.at[0]),
            pltpu.make_async_copy(theirs.at[rows], near.at[1], sems.at[1]),
            pltpu.make_async_copy(mine.at[across], far, sems.at[2]),
        ]
        for copy in found:
            copy.start()
        for copy in found:
            copy.wait()

    pl.when(core == 0)(lambda: copies(keys, values, 1))
    pl.when(core == 1)(lambda: copies(values, keys, -1))


def to_send(at, keys, values):
    rows, kv = keys.shape[0] // SIDE, keys.shape[1]
    return pl.pallas_call(
        send_kernel,
        out_shape=[
            jax.ShapeDtypeStruct((2, rows, kv), bf16),
            jax.ShapeDtypeStruct((rows, kv), bf16),
            TOKEN,
        ],
        in_specs=[SMEM] + [ANY] * 2,
        out_specs=[VMEM] * 3,
        scratch_shapes=[pltpu.SemaphoreType.DMA((3,))],
        compiler_params=params(60),
        cost_estimate=cost(0, 12 * rows * kv),
    )(at, keys, values)


def weight_sources(at, keys, values, near, near_theirs, far, far_theirs):
    core = at[2]
    found = []
    for kind in range(2):
        own = ((keys, (core + kind) % 2 == 0), (values, (core + kind) % 2 == 1))
        found.append(own)
        for piece in (near.at[kind], near_theirs.at[1 - kind], (far, far_theirs)[kind]):
            found.append(((piece, None),))
    return found


def start_weights(sources, own_rows, rows, target, sem):
    for source, condition in sources:
        if condition is None:
            pltpu.make_async_copy(source.at[rows], target, sem).start()
        else:

            @pl.when(condition)
            def _():
                pltpu.make_async_copy(source.at[own_rows], target, sem).start()


def forward_kernel(
    at, hidden, keys, values, near, near_theirs, far, far_theirs, _, o0, o1, o2, o3, done, weights, sems
):
    width = weights.shape[1]
    sources = weight_sources(at, keys, values, near, near_theirs, far, far_theirs)
    own_rows = pl.ds(pl.multiple_of(at[3] * width, 256), width)
    order = [4 * kind + k for k in range(4) for kind in range(2)]

    def start(step):
        i = order[step]
        start_weights(sources[i], own_rows, pl.ds(0, width), weights.at[i], sems.at[i])

    for step in range(4):
        start(step)
    done[...] = jnp.zeros_like(done)
    for k, out in enumerate((o0, o1, o2, o3)):
        for step in (2 * k + 4, 2 * k + 5):
            if step < len(order):
                start(step)
        for i in (k, 4 + k):
            pltpu.make_async_copy(far, weights.at[i], sems.at[i]).wait()
        both = jnp.concatenate([weights[k], weights[4 + k]], axis=1)
        total = jnp.dot(hidden[...], both, preferred_element_type=f32).astype(bf16)
        kv = both.shape[1] // 2
        out[0] = total[:, :kv]
        out[1] = total[:, kv:]


def forward(at, hidden, keys, values, pieces, after):
    rows, width = hidden.shape
    kv = keys.shape[1]
    out = jax.ShapeDtypeStruct((2, rows, kv), bf16)
    return pl.pallas_call(
        forward_kernel,
        out_shape=[out] * 4 + [TOKEN],
        in_specs=[SMEM, VMEM] + [ANY] * 7,
        out_specs=[VMEM] * 5,
        scratch_shapes=[pltpu.VMEM((8, width, kv), bf16), pltpu.SemaphoreType.DMA((8,))],
        compiler_params=params(40),
        cost_estimate=cost(SCALE * 32 * hidden.size * kv, SCALE * 32 * width * kv),
    )(at, hidden, keys, values, *pieces, after)


def backward_kernel(
    at, b0, b1, b2, b3, keys, values, near, near_theirs, far, far_theirs, sums, maps, *rest
):
    out, done, weights, back, sems = rest[-5:]
    core, z = at[2], at[3]
    kv = b0.shape[2]
    width = weights.shape[1]
    quarter = width // SIDE
    blocks, both, _ = maps.shape
    sources = weight_sources(at, keys, values, near, near_theirs, far, far_theirs)

    def load(j):
        rows = pl.ds(j * quarter, quarter)
        own_rows = pl.ds(pl.multiple_of(z * width + j * quarter, 256), quarter)
        for i in range(8):
            start_weights(sources[i], own_rows, rows, weights.at[i, rows], sems.at[8 * j + i])

    load(0)
    load(1)
    done[...] = jnp.zeros_like(done)
    for kind in range(2):
        for k, part in enumerate((b0, b1, b2, b3)):
            start = (4 * kind + k) * kv
            back[:, start : start + kv] = part[(core + kind) % 2]
    for j in range(SIDE):
        rows = pl.ds(j * quarter, quarter)
        if j + 2 < SIDE:
            load(j + 2)
        for i in range(8):
            pltpu.make_async_copy(far.at[rows], weights.at[i, rows], sems.at[8 * j + i]).wait()
        columns = slice(j * quarter, (j + 1) * quarter)
        wide = jnp.concatenate([weights[i, columns, :] for i in range(8)], axis=1)
        total = lax.dot_general(back[...], wide, NT, preferred_element_type=f32)
        tokens = total.shape[0] // blocks
        for b in range(blocks):
            block = slice(b * tokens, (b + 1) * tokens)
            out[block, columns] = (
                total[block, :]
                + lax.dot_general(
                    sums[both:, block], maps[b, :, columns], TN, preferred_element_type=f32
                )
            ).astype(bf16)


def backward(at, backs, keys, values, pieces, sums, maps, after):
    _, rows, kv = backs[0].shape
    width = keys.shape[0] // SIDE
    return pl.pallas_call(
        backward_kernel,
        out_shape=[jax.ShapeDtypeStruct((rows, width), bf16), TOKEN],
        in_specs=[SMEM] + [VMEM] * 4 + [ANY] * 6 + [VMEM] * 2 + [ANY] * len(after),
        out_specs=[VMEM] * 2,
        scratch_shapes=[
            pltpu.VMEM((8, width, kv), bf16),
            pltpu.VMEM((rows, 8 * kv), bf16),
            pltpu.SemaphoreType.DMA((32,)),
        ],
        compiler_params=params(60),
        cost_estimate=cost(SCALE * 48 * rows * width * kv, SCALE * 32 * width * kv),
    )(at, *backs, keys, values, *pieces, sums, maps, *after)


def finish_kernel(at, sums, maps, tables, t0, t1, t2, t3, _, key_out, value_out):
    core = at[2]
    blocks, both, wide = maps.shape
    rank = both // 2
    rows, kv = key_out.shape
    tokens = rows // blocks
    for b in range(blocks):
        block = slice(b * tokens, (b + 1) * tokens)
        for kind, out in enumerate((key_out, value_out)):
            first = kind * rank
            total = sum(t[(core + kind) % 2, block].astype(f32) for t in (t0, t1, t2, t3))
            total = total + adapter_scale * lax.dot_general(
                sums[first : first + rank, block],
                maps[b, first : first + rank, wide - kv :],
                TN,
                preferred_element_type=f32,
            )
            if kind == 1:
                out[block, :] = total.astype(bf16)
            else:
                for h in range(kv // HEAD):
                    lanes = slice(h * HEAD, (h + 1) * HEAD)
                    out[block, lanes] = rotated(
                        total[:, lanes], tables[0, block, :], tables[1, block, :]
                    ).astype(bf16)


def finish(at, sums, maps, tables, terms, after):
    _, rows, kv = terms[0].shape
    return pl.pallas_call(
        finish_kernel,
        out_shape=[jax.ShapeDtypeStruct((rows, kv), bf16)] * 2,
        in_specs=[SMEM] + [VMEM] * 7 + [ANY],
        out_specs=[VMEM] * 2,
        compiler_params=params(24),
        cost_estimate=cost(0, 16 * terms[0].size),
    )(at, sums, maps, tables, *terms, after)


def give_kernel(a0, a1, a2, a3, *rest):
    out = rest[-1]
    n = out.shape[0]
    out[...] = sum(a[n:].astype(f32) for a in (a0, a1, a2, a3))


def sums_kernel(at, a0, a1, a2, a3, crossed, down, up):
    core = at[2]
    n, _, width = down.shape
    wide = crossed.shape[2]
    mine = sum(a[:n].astype(f32) for a in (a0, a1, a2, a3))

    def store(first, second):
        down[:, :, :wide] = first
        down[:, :, wide:] = second[:, :, : width - wide]
        up[...] = second[:, :, width - wide :]

    pl.when(core == 0)(lambda: store(mine, crossed[...]))
    pl.when(core == 1)(lambda: store(crossed[...], mine))


def gather_sums(at, arrived, slots_here, width, after):
    _, both, wide = arrived[0].shape
    give = pl.pallas_call(
        give_kernel,
        out_shape=jax.ShapeDtypeStruct((slots_here, both, wide), f32),
        in_specs=[VMEM] * 4 + [ANY] * len(after),
        out_specs=VMEM,
        compiler_params=params(16),
        cost_estimate=cost(0, 8 * arrived[0].size),
    )(*arrived, *after)
    return pl.pallas_call(
        sums_kernel,
        out_shape=[
            jax.ShapeDtypeStruct((slots_here, both, width), f32),
            jax.ShapeDtypeStruct((slots_here, both, 2 * wide - width), f32),
        ],
        in_specs=[SMEM] + [VMEM] * 5,
        out_specs=[VMEM] * 2,
        compiler_params=params(16),
        cost_estimate=cost(0, 8 * arrived[0].size),
    )(at, *arrived, to_other_core(give))


def per_device(
    hidden,
    key_weight_frozen,
    value_weight_frozen,
    adapter_down_maps,
    adapter_up_maps,
    block_adapter_index,
    segment_document_index,
    adapter_position,
    key_gradient,
    value_gradient,
):
    width = hidden.shape[1]
    kv_here = key_weight_frozen.shape[1]
    blocks = block_adapter_index.shape[0]
    slots_here, _, rank, _ = adapter_down_maps.shape
    both = 2 * rank
    wide = width + kv_here
    quarter = width // SIDE
    dp = lax.axis_index("dp")
    z = lax.axis_index("tensor")
    core = dp % 2
    x, y = dp // 8, (dp // 2) % 4
    first = core == 0
    line = jnp.where(first, x, y)
    cross = jnp.where(first, y, x)
    at = jnp.stack([line, cross, core, z])

    half = wide // 2
    sent_near, sent_far, sent_done = to_send(at, key_weight_frozen, value_weight_frozen)
    mine_half, give_half = split_maps(
        block_adapter_index,
        at,
        adapter_down_maps.reshape(slots_here, both, width),
        adapter_up_maps.reshape(slots_here, both, kv_here),
        sent_done,
    )
    maps_chip = pack([mine_half, to_other_core(give_half)])
    maps_line = [maps_chip] + [along_line(maps_chip, d) for d in SHIFTS]
    lists_here = riding_lists(maps_line)
    lists = to_other_core(lists_here)
    segments, _ = lax.optimization_barrier((segment_document_index, maps_chip))
    tables = rope_tables(segments)
    back = turn(tables, key_gradient, value_gradient)
    picked = pick(lists, adapter_position, at, maps_line, half, blocks, (back,))
    received = [along_cross(p, d) for p, d in zip(picked, SHIFTS)]

    near = along_z_apart(sent_near, 1)
    sent_far, _ = lax.optimization_barrier((sent_far, picked[0]))
    far = along_z(sent_far, 2)
    mine_maps, give_maps = resolve(lists, adapter_position, at, maps_line, received)
    into, maps = lora(at, hidden, back, mine_maps, to_other_core(give_maps))
    near, far, _ = lax.optimization_barrier((near, far, into))
    pieces = [near, to_other_core(near), far, to_other_core(far)]
    terms = [into] + [along_z(into, d) for d in SHIFTS]
    part_mine, part_give, sums, back = parts(
        at, hidden, back, terms, blocks, (pieces[1], pieces[3])
    )
    part = pack([to_other_core(part_give), part_mine])
    *partial, forward_done = forward(
        at, hidden, key_weight_frozen, value_weight_frozen, pieces, part
    )

    part_from = [part] + [along_cross(part, d) for d in SHIFTS]
    back_later, _ = lax.optimization_barrier((back, forward_done))
    backs = [back, along_z_apart(back, 1), along_z_apart(back, -1), along_z(back_later, 2)]
    line_sums = collect(
        lists, adapter_position, at, part_from, 2 * slots_here, [forward_done] + backs[1:3]
    )
    arrived = [line_sums[0]] + [along_line(s, d) for s, d in zip(line_sums[1:], SHIFTS)]
    key_terms = [
        partial[0],
        along_z_apart(partial[1], -1),
        along_z_apart(partial[2], 1),
        along_z(partial[3], 2),
    ]
    hidden_gradient, backward_done = backward(
        at, backs, key_weight_frozen, value_weight_frozen, pieces, sums, maps, line_sums[:1]
    )
    grad_down, grad_up = gather_sums(at, arrived, slots_here, width, (backward_done,))
    key_out, value_out = finish(at, sums, maps, tables, key_terms, grad_up)
    return (
        key_out,
        value_out,
        hidden_gradient,
        grad_down.reshape(adapter_down_maps.shape),
        grad_up.reshape(adapter_up_maps.shape),
    )


def solution(mesh):
    return jax.shard_map(
        per_device,
        mesh=mesh,
        in_specs=(
            P("dp", "tensor"),
            P(None, "tensor"),
            P(None, "tensor"),
            P("dp", None, None, "tensor"),
            P("dp", None, None, "tensor"),
            P("dp"),
            P("dp", None),
            P(),
            P("dp", "tensor"),
            P("dp", "tensor"),
        ),
        out_specs=(
            P("dp", "tensor"),
            P("dp", "tensor"),
            P("dp", "tensor"),
            P("dp", None, None, "tensor"),
            P("dp", None, None, "tensor"),
        ),
        check_vma=False,
    )
```

```python
import math

import jax
import jax.numpy as jnp
from jax import lax
from jax.experimental import pallas as pl
from jax.experimental.pallas import tpu as pltpu
from jax.sharding import PartitionSpec as P

HEAD = 128
SIDE = 4
SHIFTS = (1, -1, 2)
SCALE = 1000
TOKEN = jax.ShapeDtypeStruct((8, HEAD), jnp.float32)

adapter_scale = 0.5
rope_theta = 500000.0
bf16 = jnp.bfloat16
f32 = jnp.float32
ANY = pl.BlockSpec(memory_space=pl.ANY)
VMEM = pl.BlockSpec(memory_space=pltpu.VMEM)
SMEM = pl.BlockSpec(memory_space=pltpu.SMEM)
NT = (((1,), (1,)), ((), ()))
TN = (((0,), (0,)), ((), ()))


def exchange(array, move):
    pairs = []
    for x in range(SIDE):
        for y in range(SIDE):
            for c in range(2):
                for z in range(SIDE):
                    x2, y2, c2, z2 = move(x, y, c, z)
                    target = (((x2 % SIDE) * SIDE + y2 % SIDE) * 2 + c2) * SIDE + z2 % SIDE
                    pairs.append((((x * SIDE + y) * 2 + c) * SIDE + z, target))
    return lax.ppermute(array, ("dp", "tensor"), pairs)


def along_z(array, shift):
    return exchange(array, lambda x, y, c, z: (x, y, c, z + shift))


def to_other_core(array):
    return exchange(array, lambda x, y, c, z: (x, y, 1 - c, z))


def along_z_apart(array, shift):
    return exchange(array, lambda x, y, c, z: (x, y, c, z + (shift if c == 0 else -shift)))


def along_line(array, shift):
    return exchange(
        array, lambda x, y, c, z: (x + shift, y, c, z) if c == 0 else (x, y + shift, c, z)
    )


def along_cross(array, shift):
    return exchange(
        array, lambda x, y, c, z: (x, y + shift, c, z) if c == 0 else (x + shift, y, c, z)
    )


def params(megabytes):
    return pltpu.CompilerParams(vmem_limit_bytes=megabytes << 20)


def cost(flops, moved):
    return pl.CostEstimate(flops=flops // SCALE, bytes_accessed=moved // SCALE, transcendentals=0)


def rope_tables(segments):
    places = jnp.arange(segments.shape[1], dtype=jnp.int32)
    earlier = jnp.concatenate([segments[:, :1] - 1, segments[:, :-1]], axis=1)
    starts = lax.cummax(jnp.where(segments != earlier, places[None, :], 0), axis=1)
    position = (places[None, :] - starts).astype(jnp.float32).reshape(-1)
    halves = jnp.arange(HEAD // 2, dtype=jnp.float32)
    inverse = jnp.exp(halves * (-2.0 * math.log(rope_theta) / HEAD))
    angles = position[:, None] * jnp.concatenate([inverse, inverse])[None, :]
    sign = jnp.where(jnp.arange(HEAD) < HEAD // 2, 1.0, -1.0)
    return jnp.stack([jnp.cos(angles), jnp.sin(angles) * sign[None, :]])


def unrotated(values, cosine, signed):
    return values * cosine + pltpu.roll(values, HEAD // 2, 1) * signed


def rotated(values, cosine, signed):
    return values * cosine - pltpu.roll(values, HEAD // 2, 1) * signed


def placed(slot, core):
    slot_x, slot_y = slot >> 4, (slot >> 2) & 3
    on_line = jnp.where(core == 0, slot_x, slot_y)
    on_cross = jnp.where(core == 0, slot_y, slot_x)
    row = ((slot & 3) + 2 * core) & 3
    return on_line, on_cross, row


def piece_from(here, there):
    apart = (here - there) & 3
    return jnp.where(apart == 3, 2, jnp.where(apart == 2, 3, apart))


def pack_kernel(count, *refs):
    out, sems = refs[-2], refs[-1]
    copies = []
    start = 0
    for i, piece in enumerate(refs[:count]):
        if piece.ndim < out.ndim:
            copies.append(pltpu.make_async_copy(piece, out.at[start], sems.at[i]))
            start += 1
        else:
            size = piece.shape[0]
            copies.append(pltpu.make_async_copy(piece, out.at[pl.ds(start, size)], sems.at[i]))
            start += size
    for copy in copies:
        copy.start()
    for copy in copies:
        copy.wait()


def pack(pieces, after=(), new_axis=False):
    if new_axis:
        shape = (len(pieces),) + pieces[0].shape
    else:
        shape = (sum(p.shape[0] for p in pieces),) + pieces[0].shape[1:]

    def kernel(*refs):
        pack_kernel(len(pieces), *refs)

    return pl.pallas_call(
        kernel,
        out_shape=jax.ShapeDtypeStruct(shape, pieces[0].dtype),
        in_specs=[ANY] * (len(pieces) + len(after)),
        out_specs=VMEM,
        scratch_shapes=[pltpu.SemaphoreType.DMA((len(pieces),))],
        compiler_params=params(16),
        cost_estimate=cost(0, 4 * math.prod(shape)),
    )(*pieces, *after)


def halves_kernel(index, at, down, up, _, mine, give, riding, sems):
    core = at[2]
    slots, both, width = down.shape
    wide = mine.shape[2] - HEAD
    lane = lax.broadcasted_iota(jnp.int32, riding.shape, 2)
    value = jnp.zeros(riding.shape, f32)
    for b in range(index.shape[0]):
        value = jnp.where(lane == b, index[b].astype(f32), value)
    riding[...] = value.astype(bf16)
    ends = [
        pltpu.make_async_copy(riding, out.at[:, :, pl.ds(wide, HEAD)], sems.at[i])
        for i, out in enumerate((mine, give))
    ]
    for copy in ends:
        copy.start()

    def halves(first, second):
        copies = [
            pltpu.make_async_copy(
                down.at[:, :, pl.ds(0, wide)], first.at[:, :, pl.ds(0, wide)], sems.at[2]
            ),
            pltpu.make_async_copy(
                down.at[:, :, pl.ds(wide, width - wide)],
                second.at[:, :, pl.ds(0, width - wide)],
                sems.at[3],
            ),
            pltpu.make_async_copy(
                up, second.at[:, :, pl.ds(width - wide, 2 * wide - width)], sems.at[4]
            ),
        ]
        for copy in copies:
            copy.start()
        for copy in copies:
            copy.wait()

    pl.when(core == 0)(lambda: halves(mine, give))
    pl.when(core == 1)(lambda: halves(give, mine))
    for copy in ends:
        copy.wait()


def split_maps(index, at, down, up, after):
    slots, both, width = down.shape
    wide = (width + up.shape[2]) // 2
    out = jax.ShapeDtypeStruct((slots, both, wide + HEAD), bf16)
    return pl.pallas_call(
        halves_kernel,
        out_shape=[out] * 2,
        in_specs=[SMEM] * 2 + [ANY] * 3,
        out_specs=[VMEM] * 2,
        scratch_shapes=[pltpu.VMEM((slots, both, HEAD), bf16), pltpu.SemaphoreType.DMA((5,))],
        compiler_params=params(16),
        cost_estimate=cost(0, 4 * down.size),
    )(index, at, down, up, after)


def lists_kernel(m0, m1, m2, m3, out, rows, sems):
    slots = m0.shape[0] // 2
    wide = m0.shape[2] - HEAD
    copies = [
        pltpu.make_async_copy(
            piece.at[k * slots, pl.ds(0, 16), pl.ds(wide, HEAD)], rows.at[2 * i + k], sems.at[2 * i + k]
        )
        for i, piece in enumerate((m0, m1, m2, m3))
        for k in range(2)
    ]
    for copy in copies:
        copy.start()
    for copy in copies:
        copy.wait()
    out[...] = rows[:, 0, :].astype(f32).astype(jnp.int32)


def riding_lists(pieces):
    return pl.pallas_call(
        lists_kernel,
        out_shape=jax.ShapeDtypeStruct((8, HEAD), jnp.int32),
        in_specs=[ANY] * 4,
        out_specs=VMEM,
        scratch_shapes=[pltpu.VMEM((8, 16, HEAD), bf16), pltpu.SemaphoreType.DMA((8,))],
        compiler_params=params(16),
        cost_estimate=cost(0, 1 << 16),
    )(*pieces)


def listed(lists, piece, b):
    return lists[2 * piece + b // 4, b % 4]


def pick_kernel(lists, positions, at, m0, m1, m2, m3, *rest):
    o1, o2, o3, sems = rest[-4:]
    line, cross, core = at[0], at[1], at[2]
    count, _, wide = o1.shape
    found = []
    for i, (row, out) in enumerate(((2, o1), (1, o2), (3, o3))):
        for b in range(count):
            on_line, on_cross, local = placed(positions[listed(lists, row, b)], core)
            piece = jnp.where(on_cross == cross, piece_from(line, on_line), SIDE)
            found.append((piece, out.at[b], sems.at[i * count + b]))
            for k, source in enumerate((m0, m1, m2, m3)):

                @pl.when(piece == k)
                def _():
                    pltpu.make_async_copy(
                        source.at[local, :, pl.ds(0, wide)], out.at[b], sems.at[i * count + b]
                    ).start()

    for piece, target, sem in found:

        @pl.when(piece < SIDE)
        def _():
            pltpu.make_async_copy(m0.at[0, :, pl.ds(0, wide)], target, sem).wait()


def pick(lists, positions, at, pieces, wide, blocks, after):
    count = 2 * blocks
    out = jax.ShapeDtypeStruct((count, pieces[0].shape[1], wide), bf16)
    return pl.pallas_call(
        pick_kernel,
        out_shape=[out] * 3,
        in_specs=[SMEM] * 3 + [ANY] * (4 + len(after)),
        out_specs=[VMEM] * 3,
        scratch_shapes=[pltpu.SemaphoreType.DMA((3 * count,))],
        compiler_params=params(60),
        cost_estimate=cost(0, 8 * pieces[0].size),
    )(lists, positions, at, *pieces, *after)


def start_block(lists, positions, at, line_pieces, cross_pieces, b, target, sem):
    line, cross, core = at[0], at[1], at[2]
    wide = cross_pieces[0].shape[2]
    on_line, on_cross, local = placed(positions[listed(lists, 0, b)], core)
    piece = piece_from(line, on_line)
    sender = piece_from(cross, on_cross)
    for k, source in enumerate(line_pieces):

        @pl.when((sender == 0) & (piece == k))
        def _():
            pltpu.make_async_copy(source.at[local, :, pl.ds(0, wide)], target, sem).start()

    for k, source in enumerate(cross_pieces):

        @pl.when(sender == k + 1)
        def _():
            pltpu.make_async_copy(source.at[b], target, sem).start()


def resolve_kernel(lists, positions, at, m0, m1, m2, m3, r1, r2, r3, mine, give, sems):
    blocks = mine.shape[0]
    targets = [give.at[b] for b in range(blocks)] + [mine.at[b] for b in range(blocks)]
    for b, target in enumerate(targets):
        start_block(lists, positions, at, (m0, m1, m2, m3), (r1, r2, r3), b, target, sems.at[b])
    for b, target in enumerate(targets):
        pltpu.make_async_copy(r1.at[0], target, sems.at[b]).wait()


def resolve(lists, positions, at, pieces, received):
    count, both, wide = received[0].shape
    out = jax.ShapeDtypeStruct((count // 2, both, wide), bf16)
    return pl.pallas_call(
        resolve_kernel,
        out_shape=[out] * 2,
        in_specs=[SMEM] * 3 + [ANY] * 7,
        out_specs=[VMEM] * 2,
        scratch_shapes=[pltpu.SemaphoreType.DMA((count,))],
        compiler_params=params(60),
        cost_estimate=cost(0, 2 * received[0].size),
    )(lists, positions, at, *pieces, *received)


def lora_kernel(at, hidden, back, mine, other, out, maps):
    core = at[2]
    blocks, both, _ = maps.shape
    wide = other.shape[2]
    width = hidden.shape[1]
    tokens = hidden.shape[0] // blocks

    @pl.when(core == 0)
    def _():
        maps[:, :, :wide] = mine[...]
        maps[:, :, wide:] = other[...]

    @pl.when(core == 1)
    def _():
        maps[:, :, :wide] = other[...]
        maps[:, :, wide:] = mine[...]

    half = lax.broadcasted_iota(jnp.int32, (both, tokens), 0) < both // 2
    for b in range(blocks):
        rows = pl.ds(b * tokens, tokens)
        down = maps[b, :, :width]
        up = maps[b, :, width:]
        into = lax.dot_general(down, hidden[rows, :], NT, preferred_element_type=f32)
        keys = lax.dot_general(up, back[0, rows, :], NT, preferred_element_type=f32)
        values = lax.dot_general(up, back[1, rows, :], NT, preferred_element_type=f32)
        out[:both, rows] = into.astype(bf16)
        out[both:, rows] = jnp.where(half, keys, values).astype(bf16)


def lora(at, hidden, back, mine, other):
    blocks, both, wide = other.shape
    return pl.pallas_call(
        lora_kernel,
        out_shape=[
            jax.ShapeDtypeStruct((2 * both, hidden.shape[0]), bf16),
            jax.ShapeDtypeStruct((blocks, both, 2 * wide), bf16),
        ],
        in_specs=[SMEM] + [VMEM] * 4,
        out_specs=[VMEM] * 2,
        compiler_params=params(24),
        cost_estimate=cost(2 * both * hidden.size, 2 * hidden.size + 4 * other.size),
    )(at, hidden, back, mine, other)


def parts_kernel(at, hidden, back, t0, t1, t2, t3, _1, _2, mine, give, sums, again, part):
    again[...] = back[...]
    core = at[2]
    blocks, both, _ = part.shape
    wide = mine.shape[2]
    width = hidden.shape[1]
    tokens = hidden.shape[0] // blocks
    rank = both // 2
    total = t0[...].astype(f32) + t1[...].astype(f32) + t2[...].astype(f32) + t3[...].astype(f32)
    sums[:both, :] = total[:both].astype(bf16)
    sums[both:, :] = (total[both:] * adapter_scale).astype(bf16)
    for b in range(blocks):
        rows = pl.ds(b * tokens, tokens)
        inner = sums[both:, rows]
        into = sums[:both, rows]
        down = jnp.dot(inner, hidden[rows, :], preferred_element_type=f32)
        part[b, :, :width] = down.astype(bf16)
        keys = jnp.dot(into[:rank], back[0, rows, :], preferred_element_type=f32)
        values = jnp.dot(into[rank:], back[1, rows, :], preferred_element_type=f32)
        part[b, :rank, width:] = (keys * adapter_scale).astype(bf16)
        part[b, rank:, width:] = (values * adapter_scale).astype(bf16)

    @pl.when(core == 0)
    def _():
        mine[...] = part[:, :, :wide]
        give[...] = part[:, :, wide:]

    @pl.when(core == 1)
    def _():
        mine[...] = part[:, :, wide:]
        give[...] = part[:, :, :wide]


def parts(at, hidden, back, pieces, blocks, after):
    both = pieces[0].shape[0] // 2
    wide = (hidden.shape[1] + back.shape[2]) // 2
    return pl.pallas_call(
        parts_kernel,
        out_shape=[
            jax.ShapeDtypeStruct((blocks, both, wide), bf16),
            jax.ShapeDtypeStruct((blocks, both, wide), bf16),
            jax.ShapeDtypeStruct(pieces[0].shape, bf16),
            jax.ShapeDtypeStruct(back.shape, bf16),
        ],
        in_specs=[SMEM] + [VMEM] * 6 + [ANY] * 2,
        out_specs=[VMEM] * 4,
        scratch_shapes=[pltpu.VMEM((blocks, both, 2 * wide), bf16)],
        compiler_params=params(24),
        cost_estimate=cost(2 * both * hidden.size, 4 * hidden.size),
    )(at, hidden, back, *pieces, *after)


def collect_kernel(lists, positions, at, p0, p1, p2, p3, *rest):
    o0, o1, o2, o3, total, held, sems = rest[-7:]
    line, cross, core = at[0], at[1], at[2]
    slots = o0.shape[0]
    found = []
    for i, piece in enumerate((p0, p1, p2, p3)):
        for b in range(piece.shape[0]):
            on_line, on_cross, local = placed(positions[lists[2 * i + b // 4, b % 4]], core)
            n = len(found)
            found.append((on_cross == cross, on_line * slots + local))

            @pl.when(on_cross == cross)
            def _():
                pltpu.make_async_copy(piece.at[b], held.at[n], sems.at[n]).start()

    total[...] = jnp.zeros_like(total)
    for n, (here, slot) in enumerate(found):

        @pl.when(here)
        def _():
            pltpu.make_async_copy(p0.at[0], held.at[n], sems.at[n]).wait()
            total[slot] = total[slot] + held[n].astype(f32)

    for shift, out in zip((0,) + SHIFTS, (o0, o1, o2, o3)):
        target = (line + shift + SIDE) % SIDE
        out[...] = total[pl.ds(target * slots, slots)].astype(bf16)


def collect(lists, positions, at, pieces, slots, after):
    count, both, wide = pieces[0].shape
    return pl.pallas_call(
        collect_kernel,
        out_shape=[jax.ShapeDtypeStruct((slots, both, wide), bf16)] * 4,
        in_specs=[SMEM] * 3 + [ANY] * (4 + len(after)),
        out_specs=[VMEM] * 4,
        scratch_shapes=[
            pltpu.VMEM((4 * slots, both, wide), f32),
            pltpu.VMEM((4 * count, both, wide), bf16),
            pltpu.SemaphoreType.DMA((4 * count,)),
        ],
        compiler_params=params(60),
        cost_estimate=cost(8 * pieces[0].size, 16 * pieces[0].size),
    )(lists, positions, at, *pieces, *after)


def turn_kernel(tables, key_grad, value_grad, back):
    for h in range(key_grad.shape[1] // HEAD):
        lanes = slice(h * HEAD, (h + 1) * HEAD)
        back[0, :, lanes] = unrotated(
            key_grad[:, lanes].astype(f32), tables[0], tables[1]
        ).astype(bf16)
    back[1] = value_grad[...]


def turn(tables, key_grad, value_grad):
    return pl.pallas_call(
        turn_kernel,
        out_shape=jax.ShapeDtypeStruct((2,) + key_grad.shape, bf16),
        in_specs=[VMEM] * 3,
        out_specs=VMEM,
        compiler_params=params(16),
        cost_estimate=cost(0, 10 * key_grad.size),
    )(tables, key_grad, value_grad)


def send_kernel(at, keys, values, near, far, done, sems):
    done[...] = jnp.zeros_like(done)
    core, z = at[2], at[3]
    width = far.shape[0]

    def copies(mine, theirs, shift):
        rows = pl.ds(pl.multiple_of(((z + shift + SIDE) % SIDE) * width, 256), width)
        across = pl.ds(pl.multiple_of(((z + 2) % SIDE) * width, 256), width)
        found = [
            pltpu.make_async_copy(mine.at[rows], near.at[0], sems.at[0]),
            pltpu.make_async_copy(theirs.at[rows], near.at[1], sems.at[1]),
            pltpu.make_async_copy(mine.at[across], far, sems.at[2]),
        ]
        for copy in found:
            copy.start()
        for copy in found:
            copy.wait()

    pl.when(core == 0)(lambda: copies(keys, values, 1))
    pl.when(core == 1)(lambda: copies(values, keys, -1))


def to_send(at, keys, values):
    rows, kv = keys.shape[0] // SIDE, keys.shape[1]
    return pl.pallas_call(
        send_kernel,
        out_shape=[
            jax.ShapeDtypeStruct((2, rows, kv), bf16),
            jax.ShapeDtypeStruct((rows, kv), bf16),
            TOKEN,
        ],
        in_specs=[SMEM] + [ANY] * 2,
        out_specs=[VMEM] * 3,
        scratch_shapes=[pltpu.SemaphoreType.DMA((3,))],
        compiler_params=params(60),
        cost_estimate=cost(0, 12 * rows * kv),
    )(at, keys, values)


def weight_sources(at, keys, values, near, near_theirs, far, far_theirs):
    core = at[2]
    found = []
    for kind in range(2):
        own = ((keys, (core + kind) % 2 == 0), (values, (core + kind) % 2 == 1))
        found.append(own)
        for piece in (near.at[kind], near_theirs.at[1 - kind], (far, far_theirs)[kind]):
            found.append(((piece, None),))
    return found


def start_weights(sources, own_rows, rows, target, sem):
    for source, condition in sources:
        if condition is None:
            pltpu.make_async_copy(source.at[rows], target, sem).start()
        else:

            @pl.when(condition)
            def _():
                pltpu.make_async_copy(source.at[own_rows], target, sem).start()


def forward_kernel(
    at, hidden, keys, values, near, near_theirs, far, far_theirs, _, o0, o1, o2, o3, done, weights, sems
):
    width = weights.shape[1]
    sources = weight_sources(at, keys, values, near, near_theirs, far, far_theirs)
    own_rows = pl.ds(pl.multiple_of(at[3] * width, 256), width)
    order = [4 * kind + k for k in range(4) for kind in range(2)]

    def start(step):
        i = order[step]
        start_weights(sources[i], own_rows, pl.ds(0, width), weights.at[i], sems.at[i])

    for step in range(4):
        start(step)
    done[...] = jnp.zeros_like(done)
    for k, out in enumerate((o0, o1, o2, o3)):
        for step in (2 * k + 4, 2 * k + 5):
            if step < len(order):
                start(step)
        for i in (k, 4 + k):
            pltpu.make_async_copy(far, weights.at[i], sems.at[i]).wait()
        both = jnp.concatenate([weights[k], weights[4 + k]], axis=1)
        total = jnp.dot(hidden[...], both, preferred_element_type=f32).astype(bf16)
        kv = both.shape[1] // 2
        out[0] = total[:, :kv]
        out[1] = total[:, kv:]


def forward(at, hidden, keys, values, pieces, after):
    rows, width = hidden.shape
    kv = keys.shape[1]
    out = jax.ShapeDtypeStruct((2, rows, kv), bf16)
    return pl.pallas_call(
        forward_kernel,
        out_shape=[out] * 4 + [TOKEN],
        in_specs=[SMEM, VMEM] + [ANY] * 7,
        out_specs=[VMEM] * 5,
        scratch_shapes=[pltpu.VMEM((8, width, kv), bf16), pltpu.SemaphoreType.DMA((8,))],
        compiler_params=params(40),
        cost_estimate=cost(SCALE * 32 * hidden.size * kv, SCALE * 32 * width * kv),
    )(at, hidden, keys, values, *pieces, after)


def backward_kernel(
    at, b0, b1, b2, b3, keys, values, near, near_theirs, far, far_theirs, sums, maps, *rest
):
    out, done, weights, back, sems = rest[-5:]
    core, z = at[2], at[3]
    kv = b0.shape[2]
    width = weights.shape[1]
    quarter = width // SIDE
    blocks, both, _ = maps.shape
    sources = weight_sources(at, keys, values, near, near_theirs, far, far_theirs)

    def load(j):
        rows = pl.ds(j * quarter, quarter)
        own_rows = pl.ds(pl.multiple_of(z * width + j * quarter, 256), quarter)
        for i in range(8):
            start_weights(sources[i], own_rows, rows, weights.at[i, rows], sems.at[8 * j + i])

    load(0)
    load(1)
    done[...] = jnp.zeros_like(done)
    for kind in range(2):
        for k, part in enumerate((b0, b1, b2, b3)):
            start = (4 * kind + k) * kv
            back[:, start : start + kv] = part[(core + kind) % 2]
    for j in range(SIDE):
        rows = pl.ds(j * quarter, quarter)
        if j + 2 < SIDE:
            load(j + 2)
        for i in range(8):
            pltpu.make_async_copy(far.at[rows], weights.at[i, rows], sems.at[8 * j + i]).wait()
        columns = slice(j * quarter, (j + 1) * quarter)
        wide = jnp.concatenate([weights[i, columns, :] for i in range(8)], axis=1)
        total = lax.dot_general(back[...], wide, NT, preferred_element_type=f32)
        tokens = total.shape[0] // blocks
        for b in range(blocks):
            block = slice(b * tokens, (b + 1) * tokens)
            out[block, columns] = (
                total[block, :]
                + lax.dot_general(
                    sums[both:, block], maps[b, :, columns], TN, preferred_element_type=f32
                )
            ).astype(bf16)


def backward(at, backs, keys, values, pieces, sums, maps, after):
    _, rows, kv = backs[0].shape
    width = keys.shape[0] // SIDE
    return pl.pallas_call(
        backward_kernel,
        out_shape=[jax.ShapeDtypeStruct((rows, width), bf16), TOKEN],
        in_specs=[SMEM] + [VMEM] * 4 + [ANY] * 6 + [VMEM] * 2 + [ANY] * len(after),
        out_specs=[VMEM] * 2,
        scratch_shapes=[
            pltpu.VMEM((8, width, kv), bf16),
            pltpu.VMEM((rows, 8 * kv), bf16),
            pltpu.SemaphoreType.DMA((32,)),
        ],
        compiler_params=params(60),
        cost_estimate=cost(SCALE * 48 * rows * width * kv, SCALE * 32 * width * kv),
    )(at, *backs, keys, values, *pieces, sums, maps, *after)


def finish_kernel(at, sums, maps, tables, t0, t1, t2, t3, _, key_out, value_out):
    core = at[2]
    blocks, both, wide = maps.shape
    rank = both // 2
    rows, kv = key_out.shape
    tokens = rows // blocks
    for b in range(blocks):
        block = slice(b * tokens, (b + 1) * tokens)
        for kind, out in enumerate((key_out, value_out)):
            first = kind * rank
            total = sum(t[(core + kind) % 2, block].astype(f32) for t in (t0, t1, t2, t3))
            total = total + adapter_scale * lax.dot_general(
                sums[first : first + rank, block],
                maps[b, first : first + rank, wide - kv :],
                TN,
                preferred_element_type=f32,
            )
            if kind == 1:
                out[block, :] = total.astype(bf16)
            else:
                for h in range(kv // HEAD):
                    lanes = slice(h * HEAD, (h + 1) * HEAD)
                    out[block, lanes] = rotated(
                        total[:, lanes], tables[0, block, :], tables[1, block, :]
                    ).astype(bf16)


def finish(at, sums, maps, tables, terms, after):
    _, rows, kv = terms[0].shape
    return pl.pallas_call(
        finish_kernel,
        out_shape=[jax.ShapeDtypeStruct((rows, kv), bf16)] * 2,
        in_specs=[SMEM] + [VMEM] * 7 + [ANY],
        out_specs=[VMEM] * 2,
        compiler_params=params(24),
        cost_estimate=cost(0, 16 * terms[0].size),
    )(at, sums, maps, tables, *terms, after)


def give_kernel(a0, a1, a2, a3, *rest):
    out = rest[-1]
    n = out.shape[0]
    out[...] = sum(a[n:].astype(f32) for a in (a0, a1, a2, a3))


def sums_kernel(at, a0, a1, a2, a3, crossed, down, up):
    core = at[2]
    n, _, width = down.shape
    wide = crossed.shape[2]
    mine = sum(a[:n].astype(f32) for a in (a0, a1, a2, a3))

    def store(first, second):
        down[:, :, :wide] = first
        down[:, :, wide:] = second[:, :, : width - wide]
        up[...] = second[:, :, width - wide :]

    pl.when(core == 0)(lambda: store(mine, crossed[...]))
    pl.when(core == 1)(lambda: store(crossed[...], mine))


def gather_sums(at, arrived, slots_here, width, after):
    _, both, wide = arrived[0].shape
    give = pl.pallas_call(
        give_kernel,
        out_shape=jax.ShapeDtypeStruct((slots_here, both, wide), f32),
        in_specs=[VMEM] * 4 + [ANY] * len(after),
        out_specs=VMEM,
        compiler_params=params(16),
        cost_estimate=cost(0, 8 * arrived[0].size),
    )(*arrived, *after)
    return pl.pallas_call(
        sums_kernel,
        out_shape=[
            jax.ShapeDtypeStruct((slots_here, both, width), f32),
            jax.ShapeDtypeStruct((slots_here, both, 2 * wide - width), f32),
        ],
        in_specs=[SMEM] + [VMEM] * 5,
        out_specs=[VMEM] * 2,
        compiler_params=params(16),
        cost_estimate=cost(0, 8 * arrived[0].size),
    )(at, *arrived, to_other_core(give))


def per_device(
    hidden,
    key_weight_frozen,
    value_weight_frozen,
    adapter_down_maps,
    adapter_up_maps,
    block_adapter_index,
    segment_document_index,
    adapter_position,
    key_gradient,
    value_gradient,
):
    width = hidden.shape[1]
    kv_here = key_weight_frozen.shape[1]
    blocks = block_adapter_index.shape[0]
    slots_here, _, rank, _ = adapter_down_maps.shape
    both = 2 * rank
    wide = width + kv_here
    quarter = width // SIDE
    dp = lax.axis_index("dp")
    z = lax.axis_index("tensor")
    core = dp % 2
    x, y = dp // 8, (dp // 2) % 4
    first = core == 0
    line = jnp.where(first, x, y)
    cross = jnp.where(first, y, x)
    at = jnp.stack([line, cross, core, z])

    half = wide // 2
    sent_near, sent_far, sent_done = to_send(at, key_weight_frozen, value_weight_frozen)
    mine_half, give_half = split_maps(
        block_adapter_index,
        at,
        adapter_down_maps.reshape(slots_here, both, width),
        adapter_up_maps.reshape(slots_here, both, kv_here),
        sent_done,
    )
    maps_chip = pack([mine_half, to_other_core(give_half)])
    maps_line = [maps_chip] + [along_line(maps_chip, d) for d in SHIFTS]
    lists_here = riding_lists(maps_line)
    lists = to_other_core(lists_here)
    segments, _ = lax.optimization_barrier((segment_document_index, maps_chip))
    tables = rope_tables(segments)
    back = turn(tables, key_gradient, value_gradient)
    picked = pick(lists, adapter_position, at, maps_line, half, blocks, (back,))
    received = [along_cross(p, d) for p, d in zip(picked, SHIFTS)]

    near = along_z_apart(sent_near, 1)
    sent_far, _ = lax.optimization_barrier((sent_far, lists_here))
    far = along_z(sent_far, 2)
    mine_maps, give_maps = resolve(lists, adapter_position, at, maps_line, received)
    into, maps = lora(at, hidden, back, mine_maps, to_other_core(give_maps))
    near, far, _ = lax.optimization_barrier((near, far, into))
    pieces = [near, to_other_core(near), far, to_other_core(far)]
    terms = [into] + [along_z(into, d) for d in SHIFTS]
    part_mine, part_give, sums, back = parts(
        at, hidden, back, terms, blocks, (pieces[1], pieces[3])
    )
    part = pack([to_other_core(part_give), part_mine])
    *partial, forward_done = forward(
        at, hidden, key_weight_frozen, value_weight_frozen, pieces, part
    )

    part_from = [part] + [along_cross(part, d) for d in SHIFTS]
    back_later, _ = lax.optimization_barrier((back, forward_done))
    backs = [back, along_z_apart(back, 1), along_z_apart(back, -1), along_z(back_later, 2)]
    line_sums = collect(
        lists, adapter_position, at, part_from, 2 * slots_here, [forward_done] + backs[1:3]
    )
    arrived = [line_sums[0]] + [along_line(s, d) for s, d in zip(line_sums[1:], SHIFTS)]
    key_terms = [
        partial[0],
        along_z_apart(partial[1], -1),
        along_z_apart(partial[2], 1),
        along_z(partial[3], 2),
    ]
    hidden_gradient, backward_done = backward(
        at, backs, key_weight_frozen, value_weight_frozen, pieces, sums, maps, line_sums[:1]
    )
    grad_down, grad_up = gather_sums(at, arrived, slots_here, width, (backward_done,))
    key_out, value_out = finish(at, sums, maps, tables, key_terms, grad_up)
    return (
        key_out,
        value_out,
        hidden_gradient,
        grad_down.reshape(adapter_down_maps.shape),
        grad_up.reshape(adapter_up_maps.shape),
    )


def solution(mesh):
    return jax.shard_map(
        per_device,
        mesh=mesh,
        in_specs=(
            P("dp", "tensor"),
            P(None, "tensor"),
            P(None, "tensor"),
            P("dp", None, None, "tensor"),
            P("dp", None, None, "tensor"),
            P("dp"),
            P("dp", None),
            P(),
            P("dp", "tensor"),
            P("dp", "tensor"),
        ),
        out_specs=(
            P("dp", "tensor"),
            P("dp", "tensor"),
            P("dp", "tensor"),
            P("dp", None, None, "tensor"),
            P("dp", None, None, "tensor"),
        ),
        check_vma=False,
    )
```

```python
import math

import jax
import jax.numpy as jnp
from jax import lax
from jax.experimental import pallas as pl
from jax.experimental.pallas import tpu as pltpu
from jax.sharding import PartitionSpec as P

HEAD = 128
SIDE = 4
SHIFTS = (1, -1, 2)
SCALE = 1000
TOKEN = jax.ShapeDtypeStruct((8, HEAD), jnp.float32)

adapter_scale = 0.5
rope_theta = 500000.0
bf16 = jnp.bfloat16
f32 = jnp.float32
ANY = pl.BlockSpec(memory_space=pl.ANY)
VMEM = pl.BlockSpec(memory_space=pltpu.VMEM)
SMEM = pl.BlockSpec(memory_space=pltpu.SMEM)
NT = (((1,), (1,)), ((), ()))
TN = (((0,), (0,)), ((), ()))


def exchange(array, move):
    pairs = []
    for x in range(SIDE):
        for y in range(SIDE):
            for c in range(2):
                for z in range(SIDE):
                    x2, y2, c2, z2 = move(x, y, c, z)
                    target = (((x2 % SIDE) * SIDE + y2 % SIDE) * 2 + c2) * SIDE + z2 % SIDE
                    pairs.append((((x * SIDE + y) * 2 + c) * SIDE + z, target))
    return lax.ppermute(array, ("dp", "tensor"), pairs)


def along_z(array, shift):
    return exchange(array, lambda x, y, c, z: (x, y, c, z + shift))


def to_other_core(array):
    return exchange(array, lambda x, y, c, z: (x, y, 1 - c, z))


def along_z_apart(array, shift):
    return exchange(array, lambda x, y, c, z: (x, y, c, z + (shift if c == 0 else -shift)))


def along_line(array, shift):
    return exchange(
        array, lambda x, y, c, z: (x + shift, y, c, z) if c == 0 else (x, y + shift, c, z)
    )


def along_cross(array, shift):
    return exchange(
        array, lambda x, y, c, z: (x, y + shift, c, z) if c == 0 else (x + shift, y, c, z)
    )


def params(megabytes):
    return pltpu.CompilerParams(vmem_limit_bytes=megabytes << 20)


def cost(flops, moved):
    return pl.CostEstimate(flops=flops // SCALE, bytes_accessed=moved // SCALE, transcendentals=0)


def rope_tables(segments):
    places = jnp.arange(segments.shape[1], dtype=jnp.int32)
    earlier = jnp.concatenate([segments[:, :1] - 1, segments[:, :-1]], axis=1)
    starts = lax.cummax(jnp.where(segments != earlier, places[None, :], 0), axis=1)
    position = (places[None, :] - starts).astype(jnp.float32).reshape(-1)
    halves = jnp.arange(HEAD // 2, dtype=jnp.float32)
    inverse = jnp.exp(halves * (-2.0 * math.log(rope_theta) / HEAD))
    angles = position[:, None] * jnp.concatenate([inverse, inverse])[None, :]
    sign = jnp.where(jnp.arange(HEAD) < HEAD // 2, 1.0, -1.0)
    return jnp.stack([jnp.cos(angles), jnp.sin(angles) * sign[None, :]])


def unrotated(values, cosine, signed):
    return values * cosine + pltpu.roll(values, HEAD // 2, 1) * signed


def rotated(values, cosine, signed):
    return values * cosine - pltpu.roll(values, HEAD // 2, 1) * signed


def placed(slot, core):
    slot_x, slot_y = slot >> 4, (slot >> 2) & 3
    on_line = jnp.where(core == 0, slot_x, slot_y)
    on_cross = jnp.where(core == 0, slot_y, slot_x)
    row = ((slot & 3) + 2 * core) & 3
    return on_line, on_cross, row


def piece_from(here, there):
    apart = (here - there) & 3
    return jnp.where(apart == 3, 2, jnp.where(apart == 2, 3, apart))


def pack_kernel(count, *refs):
    out, sems = refs[-2], refs[-1]
    copies = []
    start = 0
    for i, piece in enumerate(refs[:count]):
        if piece.ndim < out.ndim:
            copies.append(pltpu.make_async_copy(piece, out.at[start], sems.at[i]))
            start += 1
        else:
            size = piece.shape[0]
            copies.append(pltpu.make_async_copy(piece, out.at[pl.ds(start, size)], sems.at[i]))
            start += size
    for copy in copies:
        copy.start()
    for copy in copies:
        copy.wait()


def pack(pieces, after=(), new_axis=False):
    if new_axis:
        shape = (len(pieces),) + pieces[0].shape
    else:
        shape = (sum(p.shape[0] for p in pieces),) + pieces[0].shape[1:]

    def kernel(*refs):
        pack_kernel(len(pieces), *refs)

    return pl.pallas_call(
        kernel,
        out_shape=jax.ShapeDtypeStruct(shape, pieces[0].dtype),
        in_specs=[ANY] * (len(pieces) + len(after)),
        out_specs=VMEM,
        scratch_shapes=[pltpu.SemaphoreType.DMA((len(pieces),))],
        compiler_params=params(16),
        cost_estimate=cost(0, 4 * math.prod(shape)),
    )(*pieces, *after)


def halves_kernel(index, positions, at, down, up, _, mine, give, riding, sems):
    core = at[2]
    slots, both, width = down.shape
    wide = mine.shape[2] - HEAD
    lane = lax.broadcasted_iota(jnp.int32, riding.shape, 2)
    value = jnp.zeros(riding.shape, f32)
    for b in range(index.shape[0]):
        value = jnp.where(lane == b, positions[index[b]].astype(f32), value)
    riding[...] = value.astype(bf16)
    ends = [
        pltpu.make_async_copy(riding, out.at[:, :, pl.ds(wide, HEAD)], sems.at[i])
        for i, out in enumerate((mine, give))
    ]
    for copy in ends:
        copy.start()

    def halves(first, second):
        copies = [
            pltpu.make_async_copy(
                down.at[:, :, pl.ds(0, wide)], first.at[:, :, pl.ds(0, wide)], sems.at[2]
            ),
            pltpu.make_async_copy(
                down.at[:, :, pl.ds(wide, width - wide)],
                second.at[:, :, pl.ds(0, width - wide)],
                sems.at[3],
            ),
            pltpu.make_async_copy(
                up, second.at[:, :, pl.ds(width - wide, 2 * wide - width)], sems.at[4]
            ),
        ]
        for copy in copies:
            copy.start()
        for copy in copies:
            copy.wait()

    pl.when(core == 0)(lambda: halves(mine, give))
    pl.when(core == 1)(lambda: halves(give, mine))
    for copy in ends:
        copy.wait()


def split_maps(index, positions, at, down, up, after):
    slots, both, width = down.shape
    wide = (width + up.shape[2]) // 2
    out = jax.ShapeDtypeStruct((slots, both, wide + HEAD), bf16)
    return pl.pallas_call(
        halves_kernel,
        out_shape=[out] * 2,
        in_specs=[SMEM] * 3 + [ANY] * 3,
        out_specs=[VMEM] * 2,
        scratch_shapes=[pltpu.VMEM((slots, both, HEAD), bf16), pltpu.SemaphoreType.DMA((5,))],
        compiler_params=params(16),
        cost_estimate=cost(0, 4 * down.size),
    )(index, positions, at, down, up, after)


def lists_kernel(m0, m1, m2, m3, out, rows, sems):
    slots = m0.shape[0] // 2
    wide = m0.shape[2] - HEAD
    copies = [
        pltpu.make_async_copy(
            piece.at[k * slots, pl.ds(0, 16), pl.ds(wide, HEAD)], rows.at[2 * i + k], sems.at[2 * i + k]
        )
        for i, piece in enumerate((m0, m1, m2, m3))
        for k in range(2)
    ]
    for copy in copies:
        copy.start()
    for copy in copies:
        copy.wait()
    out[...] = rows[:, 0, :].astype(f32).astype(jnp.int32)


def riding_lists(pieces):
    return pl.pallas_call(
        lists_kernel,
        out_shape=jax.ShapeDtypeStruct((8, HEAD), jnp.int32),
        in_specs=[ANY] * 4,
        out_specs=VMEM,
        scratch_shapes=[pltpu.VMEM((8, 16, HEAD), bf16), pltpu.SemaphoreType.DMA((8,))],
        compiler_params=params(16),
        cost_estimate=cost(0, 1 << 16),
    )(*pieces)


def listed(lists, piece, b):
    return lists[2 * piece + b // 4, b % 4]


def pick_kernel(lists, at, m0, m1, m2, m3, *rest):
    o1, o2, o3, held, sems = rest[-5:]
    line, cross, core = at[0], at[1], at[2]
    count, _, wide = o1.shape
    found = []
    for i, (row, out) in enumerate(((2, o1), (1, o2), (3, o3))):
        for b in range(count):
            n = len(found)
            on_line, on_cross, local = placed(listed(lists, row, b), core)
            piece = jnp.where(on_cross == cross, piece_from(line, on_line), SIDE)
            found.append((piece < SIDE, out.at[b]))
            for k, source in enumerate((m0, m1, m2, m3)):

                @pl.when(piece == k)
                def _():
                    pltpu.make_async_copy(
                        source.at[local, :, pl.ds(0, wide)], held.at[n], sems.at[0, n]
                    ).start()

    for n, (here, target) in enumerate(found):

        @pl.when(here)
        def _():
            pltpu.make_async_copy(m0.at[0, :, pl.ds(0, wide)], held.at[n], sems.at[0, n]).wait()
            pltpu.make_async_copy(held.at[n], target, sems.at[1, n]).start()

    for n, (here, target) in enumerate(found):

        @pl.when(here)
        def _():
            pltpu.make_async_copy(held.at[n], target, sems.at[1, n]).wait()


def pick(lists, at, pieces, wide, blocks, after):
    count = 2 * blocks
    both = pieces[0].shape[1]
    out = jax.ShapeDtypeStruct((count, both, wide), bf16)
    return pl.pallas_call(
        pick_kernel,
        out_shape=[out] * 3,
        in_specs=[SMEM] * 2 + [ANY] * (4 + len(after)),
        out_specs=[ANY] * 3,
        scratch_shapes=[
            pltpu.VMEM((3 * count, both, wide), bf16),
            pltpu.SemaphoreType.DMA((2, 3 * count)),
        ],
        compiler_params=params(63),
        cost_estimate=cost(0, 8 * pieces[0].size),
    )(lists, at, *pieces, *after)


def start_block(lists, at, line_pieces, cross_pieces, b, target, sem):
    line, cross, core = at[0], at[1], at[2]
    wide = cross_pieces[0].shape[2]
    on_line, on_cross, local = placed(listed(lists, 0, b), core)
    piece = piece_from(line, on_line)
    sender = piece_from(cross, on_cross)
    for k, source in enumerate(line_pieces):

        @pl.when((sender == 0) & (piece == k))
        def _():
            pltpu.make_async_copy(source.at[local, :, pl.ds(0, wide)], target, sem).start()

    for k, source in enumerate(cross_pieces):

        @pl.when(sender == k + 1)
        def _():
            pltpu.make_async_copy(source.at[b], target, sem).start()


def resolve_kernel(lists, at, m0, m1, m2, m3, r1, r2, r3, mine, give, sems):
    blocks = mine.shape[0]
    targets = [give.at[b] for b in range(blocks)] + [mine.at[b] for b in range(blocks)]
    for b, target in enumerate(targets):
        start_block(lists, at, (m0, m1, m2, m3), (r1, r2, r3), b, target, sems.at[b])
    for b, target in enumerate(targets):
        pltpu.make_async_copy(r1.at[0], target, sems.at[b]).wait()


def resolve(lists, at, pieces, received):
    count, both, wide = received[0].shape
    out = jax.ShapeDtypeStruct((count // 2, both, wide), bf16)
    return pl.pallas_call(
        resolve_kernel,
        out_shape=[out] * 2,
        in_specs=[SMEM] * 2 + [ANY] * 7,
        out_specs=[VMEM] * 2,
        scratch_shapes=[pltpu.SemaphoreType.DMA((count,))],
        compiler_params=params(60),
        cost_estimate=cost(0, 2 * received[0].size),
    )(lists, at, *pieces, *received)


def lora_kernel(at, hidden, back, mine, other, out, maps):
    core = at[2]
    blocks, both, _ = maps.shape
    wide = other.shape[2]
    width = hidden.shape[1]
    tokens = hidden.shape[0] // blocks

    @pl.when(core == 0)
    def _():
        maps[:, :, :wide] = mine[...]
        maps[:, :, wide:] = other[...]

    @pl.when(core == 1)
    def _():
        maps[:, :, :wide] = other[...]
        maps[:, :, wide:] = mine[...]

    half = lax.broadcasted_iota(jnp.int32, (both, tokens), 0) < both // 2
    for b in range(blocks):
        rows = pl.ds(b * tokens, tokens)
        down = maps[b, :, :width]
        up = maps[b, :, width:]
        into = lax.dot_general(down, hidden[rows, :], NT, preferred_element_type=f32)
        keys = lax.dot_general(up, back[0, rows, :], NT, preferred_element_type=f32)
        values = lax.dot_general(up, back[1, rows, :], NT, preferred_element_type=f32)
        out[:both, rows] = into.astype(bf16)
        out[both:, rows] = jnp.where(half, keys, values).astype(bf16)


def lora(at, hidden, back, mine, other):
    blocks, both, wide = other.shape
    return pl.pallas_call(
        lora_kernel,
        out_shape=[
            jax.ShapeDtypeStruct((2 * both, hidden.shape[0]), bf16),
            jax.ShapeDtypeStruct((blocks, both, 2 * wide), bf16),
        ],
        in_specs=[SMEM] + [VMEM] * 4,
        out_specs=[VMEM] * 2,
        compiler_params=params(24),
        cost_estimate=cost(2 * both * hidden.size, 2 * hidden.size + 4 * other.size),
    )(at, hidden, back, mine, other)


def parts_kernel(at, hidden, back, t0, t1, t2, t3, _1, _2, mine, give, sums, again, part):
    again[...] = back[...]
    core = at[2]
    blocks, both, _ = part.shape
    wide = mine.shape[2]
    width = hidden.shape[1]
    tokens = hidden.shape[0] // blocks
    rank = both // 2
    total = t0[...].astype(f32) + t1[...].astype(f32) + t2[...].astype(f32) + t3[...].astype(f32)
    sums[:both, :] = total[:both].astype(bf16)
    sums[both:, :] = (total[both:] * adapter_scale).astype(bf16)
    for b in range(blocks):
        rows = pl.ds(b * tokens, tokens)
        inner = sums[both:, rows]
        into = sums[:both, rows]
        down = jnp.dot(inner, hidden[rows, :], preferred_element_type=f32)
        part[b, :, :width] = down.astype(bf16)
        keys = jnp.dot(into[:rank], back[0, rows, :], preferred_element_type=f32)
        values = jnp.dot(into[rank:], back[1, rows, :], preferred_element_type=f32)
        part[b, :rank, width:] = (keys * adapter_scale).astype(bf16)
        part[b, rank:, width:] = (values * adapter_scale).astype(bf16)

    @pl.when(core == 0)
    def _():
        mine[...] = part[:, :, :wide]
        give[...] = part[:, :, wide:]

    @pl.when(core == 1)
    def _():
        mine[...] = part[:, :, wide:]
        give[...] = part[:, :, :wide]


def parts(at, hidden, back, pieces, blocks, after):
    both = pieces[0].shape[0] // 2
    wide = (hidden.shape[1] + back.shape[2]) // 2
    return pl.pallas_call(
        parts_kernel,
        out_shape=[
            jax.ShapeDtypeStruct((blocks, both, wide), bf16),
            jax.ShapeDtypeStruct((blocks, both, wide), bf16),
            jax.ShapeDtypeStruct(pieces[0].shape, bf16),
            jax.ShapeDtypeStruct(back.shape, bf16),
        ],
        in_specs=[SMEM] + [VMEM] * 6 + [ANY] * 2,
        out_specs=[VMEM] * 4,
        scratch_shapes=[pltpu.VMEM((blocks, both, 2 * wide), bf16)],
        compiler_params=params(24),
        cost_estimate=cost(2 * both * hidden.size, 4 * hidden.size),
    )(at, hidden, back, *pieces, *after)


def collect_kernel(lists, at, p0, p1, p2, p3, *rest):
    o0, o1, o2, o3, total, held, sems = rest[-7:]
    line, cross, core = at[0], at[1], at[2]
    slots = o0.shape[0]
    found = []
    for i, piece in enumerate((p0, p1, p2, p3)):
        for b in range(piece.shape[0]):
            on_line, on_cross, local = placed(listed(lists, i, b), core)
            n = len(found)
            found.append((on_cross == cross, on_line * slots + local))

            @pl.when(on_cross == cross)
            def _():
                pltpu.make_async_copy(piece.at[b], held.at[n], sems.at[n]).start()

    total[...] = jnp.zeros_like(total)
    for n, (here, slot) in enumerate(found):

        @pl.when(here)
        def _():
            pltpu.make_async_copy(p0.at[0], held.at[n], sems.at[n]).wait()
            total[slot] = total[slot] + held[n].astype(f32)

    for shift, out in zip((0,) + SHIFTS, (o0, o1, o2, o3)):
        target = (line + shift + SIDE) % SIDE
        out[...] = total[pl.ds(target * slots, slots)].astype(bf16)


def collect(lists, at, pieces, slots, after):
    count, both, wide = pieces[0].shape
    return pl.pallas_call(
        collect_kernel,
        out_shape=[jax.ShapeDtypeStruct((slots, both, wide), bf16)] * 4,
        in_specs=[SMEM] * 2 + [ANY] * (4 + len(after)),
        out_specs=[VMEM] * 4,
        scratch_shapes=[
            pltpu.VMEM((4 * slots, both, wide), f32),
            pltpu.VMEM((4 * count, both, wide), bf16),
            pltpu.SemaphoreType.DMA((4 * count,)),
        ],
        compiler_params=params(60),
        cost_estimate=cost(8 * pieces[0].size, 16 * pieces[0].size),
    )(lists, at, *pieces, *after)


def turn_kernel(tables, key_grad, value_grad, back):
    for h in range(key_grad.shape[1] // HEAD):
        lanes = slice(h * HEAD, (h + 1) * HEAD)
        back[0, :, lanes] = unrotated(
            key_grad[:, lanes].astype(f32), tables[0], tables[1]
        ).astype(bf16)
    back[1] = value_grad[...]


def turn(tables, key_grad, value_grad):
    return pl.pallas_call(
        turn_kernel,
        out_shape=jax.ShapeDtypeStruct((2,) + key_grad.shape, bf16),
        in_specs=[VMEM] * 3,
        out_specs=VMEM,
        compiler_params=params(16),
        cost_estimate=cost(0, 10 * key_grad.size),
    )(tables, key_grad, value_grad)


def send_kernel(at, keys, values, near, far, done, held, sems):
    core, z = at[2], at[3]
    width = far.shape[0]
    size = held.shape[1]
    parts = width // size
    done[...] = jnp.zeros_like(done)

    def copies(mine, theirs, shift):
        rows = ((z + shift + SIDE) % SIDE) * width
        across = ((z + 2) % SIDE) * width
        loads, saves = [], []
        for source, start, target in (
            (mine, rows, near.at[0]), (theirs, rows, near.at[1]), (mine, across, far)
        ):
            for i in range(parts):
                n = len(loads)
                here = pl.ds(pl.multiple_of(start + i * size, 256), size)
                loads.append(pltpu.make_async_copy(source.at[here], held.at[n], sems.at[0, n]))
                saves.append(
                    pltpu.make_async_copy(
                        held.at[n], target.at[pl.ds(i * size, size)], sems.at[1, n]
                    )
                )
        for copy in loads:
            copy.start()
        for load, save in zip(loads, saves):
            load.wait()
            save.start()
        for copy in saves:
            copy.wait()

    pl.when(core == 0)(lambda: copies(keys, values, 1))
    pl.when(core == 1)(lambda: copies(values, keys, -1))


def to_send(at, keys, values):
    rows, kv = keys.shape[0] // SIDE, keys.shape[1]
    size = rows // 4
    return pl.pallas_call(
        send_kernel,
        out_shape=[
            jax.ShapeDtypeStruct((2, rows, kv), bf16),
            jax.ShapeDtypeStruct((rows, kv), bf16),
            TOKEN,
        ],
        in_specs=[SMEM] + [ANY] * 2,
        out_specs=[ANY] * 2 + [VMEM],
        scratch_shapes=[pltpu.VMEM((12, size, kv), bf16), pltpu.SemaphoreType.DMA((2, 12))],
        compiler_params=params(63),
        cost_estimate=cost(0, 12 * rows * kv),
    )(at, keys, values)


def weight_sources(at, keys, values, near, near_theirs, far, far_theirs):
    core = at[2]
    found = []
    for kind in range(2):
        own = ((keys, (core + kind) % 2 == 0), (values, (core + kind) % 2 == 1))
        found.append(own)
        for piece in (near.at[kind], near_theirs.at[1 - kind], (far, far_theirs)[kind]):
            found.append(((piece, None),))
    return found


def start_weights(sources, own_rows, rows, target, sem):
    for source, condition in sources:
        if condition is None:
            pltpu.make_async_copy(source.at[rows], target, sem).start()
        else:

            @pl.when(condition)
            def _():
                pltpu.make_async_copy(source.at[own_rows], target, sem).start()


def forward_kernel(
    at, hidden, keys, values, near, near_theirs, far, far_theirs, _, o0, o1, o2, o3, done, weights, sems
):
    width = weights.shape[1]
    sources = weight_sources(at, keys, values, near, near_theirs, far, far_theirs)
    own_rows = pl.ds(pl.multiple_of(at[3] * width, 256), width)
    order = [4 * kind + k for k in range(4) for kind in range(2)]

    def start(step):
        i = order[step]
        start_weights(sources[i], own_rows, pl.ds(0, width), weights.at[i], sems.at[i])

    for step in range(4):
        start(step)
    done[...] = jnp.zeros_like(done)
    for k, out in enumerate((o0, o1, o2, o3)):
        for step in (2 * k + 4, 2 * k + 5):
            if step < len(order):
                start(step)
        for i in (k, 4 + k):
            pltpu.make_async_copy(far, weights.at[i], sems.at[i]).wait()
        both = jnp.concatenate([weights[k], weights[4 + k]], axis=1)
        total = jnp.dot(hidden[...], both, preferred_element_type=f32).astype(bf16)
        kv = both.shape[1] // 2
        out[0] = total[:, :kv]
        out[1] = total[:, kv:]


def forward(at, hidden, keys, values, pieces, after):
    rows, width = hidden.shape
    kv = keys.shape[1]
    out = jax.ShapeDtypeStruct((2, rows, kv), bf16)
    return pl.pallas_call(
        forward_kernel,
        out_shape=[out] * 4 + [TOKEN],
        in_specs=[SMEM, VMEM] + [ANY] * 7,
        out_specs=[VMEM] * 5,
        scratch_shapes=[pltpu.VMEM((8, width, kv), bf16), pltpu.SemaphoreType.DMA((8,))],
        compiler_params=params(40),
        cost_estimate=cost(SCALE * 32 * hidden.size * kv, SCALE * 32 * width * kv),
    )(at, hidden, keys, values, *pieces, after)


def backward_kernel(
    at, b0, b1, b2, b3, keys, values, near, near_theirs, far, far_theirs, sums, maps, *rest
):
    out, done, weights, back, sems = rest[-5:]
    core, z = at[2], at[3]
    kv = b0.shape[2]
    width = weights.shape[1]
    quarter = width // SIDE
    blocks, both, _ = maps.shape
    sources = weight_sources(at, keys, values, near, near_theirs, far, far_theirs)

    def load(j):
        rows = pl.ds(j * quarter, quarter)
        own_rows = pl.ds(pl.multiple_of(z * width + j * quarter, 256), quarter)
        for i in range(8):
            start_weights(sources[i], own_rows, rows, weights.at[i, rows], sems.at[8 * j + i])

    load(0)
    load(1)
    done[...] = jnp.zeros_like(done)
    for kind in range(2):
        for k, part in enumerate((b0, b1, b2, b3)):
            start = (4 * kind + k) * kv
            back[:, start : start + kv] = part[(core + kind) % 2]
    for j in range(SIDE):
        rows = pl.ds(j * quarter, quarter)
        if j + 2 < SIDE:
            load(j + 2)
        for i in range(8):
            pltpu.make_async_copy(far.at[rows], weights.at[i, rows], sems.at[8 * j + i]).wait()
        columns = slice(j * quarter, (j + 1) * quarter)
        wide = jnp.concatenate([weights[i, columns, :] for i in range(8)], axis=1)
        total = lax.dot_general(back[...], wide, NT, preferred_element_type=f32)
        tokens = total.shape[0] // blocks
        for b in range(blocks):
            block = slice(b * tokens, (b + 1) * tokens)
            out[block, columns] = (
                total[block, :]
                + lax.dot_general(
                    sums[both:, block], maps[b, :, columns], TN, preferred_element_type=f32
                )
            ).astype(bf16)


def backward(at, backs, keys, values, pieces, sums, maps, after):
    _, rows, kv = backs[0].shape
    width = keys.shape[0] // SIDE
    return pl.pallas_call(
        backward_kernel,
        out_shape=[jax.ShapeDtypeStruct((rows, width), bf16), TOKEN],
        in_specs=[SMEM] + [VMEM] * 4 + [ANY] * 6 + [VMEM] * 2 + [ANY] * len(after),
        out_specs=[VMEM] * 2,
        scratch_shapes=[
            pltpu.VMEM((8, width, kv), bf16),
            pltpu.VMEM((rows, 8 * kv), bf16),
            pltpu.SemaphoreType.DMA((32,)),
        ],
        compiler_params=params(60),
        cost_estimate=cost(SCALE * 48 * rows * width * kv, SCALE * 32 * width * kv),
    )(at, *backs, keys, values, *pieces, sums, maps, *after)


def finish_kernel(at, sums, maps, tables, t0, t1, t2, t3, _, key_out, value_out):
    core = at[2]
    blocks, both, wide = maps.shape
    rank = both // 2
    rows, kv = key_out.shape
    tokens = rows // blocks
    for b in range(blocks):
        block = slice(b * tokens, (b + 1) * tokens)
        for kind, out in enumerate((key_out, value_out)):
            first = kind * rank
            total = sum(t[(core + kind) % 2, block].astype(f32) for t in (t0, t1, t2, t3))
            total = total + adapter_scale * lax.dot_general(
                sums[first : first + rank, block],
                maps[b, first : first + rank, wide - kv :],
                TN,
                preferred_element_type=f32,
            )
            if kind == 1:
                out[block, :] = total.astype(bf16)
            else:
                for h in range(kv // HEAD):
                    lanes = slice(h * HEAD, (h + 1) * HEAD)
                    out[block, lanes] = rotated(
                        total[:, lanes], tables[0, block, :], tables[1, block, :]
                    ).astype(bf16)


def finish(at, sums, maps, tables, terms, after):
    _, rows, kv = terms[0].shape
    return pl.pallas_call(
        finish_kernel,
        out_shape=[jax.ShapeDtypeStruct((rows, kv), bf16)] * 2,
        in_specs=[SMEM] + [VMEM] * 7 + [ANY],
        out_specs=[VMEM] * 2,
        compiler_params=params(24),
        cost_estimate=cost(0, 16 * terms[0].size),
    )(at, sums, maps, tables, *terms, after)


def give_kernel(a0, a1, a2, a3, *rest):
    out = rest[-1]
    n = out.shape[0]
    out[...] = sum(a[n:].astype(f32) for a in (a0, a1, a2, a3))


def sums_kernel(at, a0, a1, a2, a3, crossed, down, up):
    core = at[2]
    n, _, width = down.shape
    wide = crossed.shape[2]
    mine = sum(a[:n].astype(f32) for a in (a0, a1, a2, a3))

    def store(first, second):
        down[:, :, :wide] = first
        down[:, :, wide:] = second[:, :, : width - wide]
        up[...] = second[:, :, width - wide :]

    pl.when(core == 0)(lambda: store(mine, crossed[...]))
    pl.when(core == 1)(lambda: store(crossed[...], mine))


def gather_sums(at, arrived, slots_here, width, after):
    _, both, wide = arrived[0].shape
    give = pl.pallas_call(
        give_kernel,
        out_shape=jax.ShapeDtypeStruct((slots_here, both, wide), f32),
        in_specs=[VMEM] * 4 + [ANY] * len(after),
        out_specs=VMEM,
        compiler_params=params(16),
        cost_estimate=cost(0, 8 * arrived[0].size),
    )(*arrived, *after)
    return pl.pallas_call(
        sums_kernel,
        out_shape=[
            jax.ShapeDtypeStruct((slots_here, both, width), f32),
            jax.ShapeDtypeStruct((slots_here, both, 2 * wide - width), f32),
        ],
        in_specs=[SMEM] + [VMEM] * 5,
        out_specs=[VMEM] * 2,
        compiler_params=params(16),
        cost_estimate=cost(0, 8 * arrived[0].size),
    )(at, *arrived, to_other_core(give))


def per_device(
    hidden,
    key_weight_frozen,
    value_weight_frozen,
    adapter_down_maps,
    adapter_up_maps,
    block_adapter_index,
    segment_document_index,
    adapter_position,
    key_gradient,
    value_gradient,
):
    width = hidden.shape[1]
    kv_here = key_weight_frozen.shape[1]
    blocks = block_adapter_index.shape[0]
    slots_here, _, rank, _ = adapter_down_maps.shape
    both = 2 * rank
    wide = width + kv_here
    quarter = width // SIDE
    dp = lax.axis_index("dp")
    z = lax.axis_index("tensor")
    core = dp % 2
    x, y = dp // 8, (dp // 2) % 4
    first = core == 0
    line = jnp.where(first, x, y)
    cross = jnp.where(first, y, x)
    at = jnp.stack([line, cross, core, z])

    half = wide // 2
    sent_near, sent_far, sent_done = to_send(at, key_weight_frozen, value_weight_frozen)
    mine_half, give_half = split_maps(
        block_adapter_index,
        adapter_position,
        at,
        adapter_down_maps.reshape(slots_here, both, width),
        adapter_up_maps.reshape(slots_here, both, kv_here),
        sent_done,
    )
    maps_chip = pack([mine_half, to_other_core(give_half)])
    maps_line = [maps_chip] + [along_line(maps_chip, d) for d in SHIFTS]
    lists_here = riding_lists(maps_line)
    lists = to_other_core(lists_here)
    segments, _ = lax.optimization_barrier((segment_document_index, maps_chip))
    tables = rope_tables(segments)
    back = turn(tables, key_gradient, value_gradient)
    picked = pick(lists, at, maps_line, half, blocks, (back,))
    received = [along_cross(p, d) for p, d in zip(picked, SHIFTS)]

    near = along_z_apart(sent_near, 1)
    sent_far, _ = lax.optimization_barrier((sent_far, lists_here))
    far = along_z(sent_far, 2)
    mine_maps, give_maps = resolve(lists, at, maps_line, received)
    into, maps = lora(at, hidden, back, mine_maps, to_other_core(give_maps))
    near, far, _ = lax.optimization_barrier((near, far, into))
    pieces = [near, to_other_core(near), far, to_other_core(far)]
    terms = [into] + [along_z(into, d) for d in SHIFTS]
    part_mine, part_give, sums, back = parts(
        at, hidden, back, terms, blocks, (pieces[1], pieces[3])
    )
    part = pack([to_other_core(part_give), part_mine])
    *partial, forward_done = forward(
        at, hidden, key_weight_frozen, value_weight_frozen, pieces, part
    )

    part_from = [part] + [along_cross(part, d) for d in SHIFTS]
    back_later, _ = lax.optimization_barrier((back, forward_done))
    backs = [back, along_z_apart(back, 1), along_z_apart(back, -1), along_z(back_later, 2)]
    line_sums = collect(
        lists, at, part_from, 2 * slots_here, [forward_done] + backs[1:3]
    )
    arrived = [line_sums[0]] + [along_line(s, d) for s, d in zip(line_sums[1:], SHIFTS)]
    key_terms = [
        partial[0],
        along_z_apart(partial[1], -1),
        along_z_apart(partial[2], 1),
        along_z(partial[3], 2),
    ]
    hidden_gradient, backward_done = backward(
        at, backs, key_weight_frozen, value_weight_frozen, pieces, sums, maps,
        line_sums[:1],
    )
    grad_down, grad_up = gather_sums(at, arrived, slots_here, width, (backward_done,))
    key_out, value_out = finish(at, sums, maps, tables, key_terms, grad_up)
    return (
        key_out,
        value_out,
        hidden_gradient,
        grad_down.reshape(adapter_down_maps.shape),
        grad_up.reshape(adapter_up_maps.shape),
    )


def solution(mesh):
    return jax.shard_map(
        per_device,
        mesh=mesh,
        in_specs=(
            P("dp", "tensor"),
            P(None, "tensor"),
            P(None, "tensor"),
            P("dp", None, None, "tensor"),
            P("dp", None, None, "tensor"),
            P("dp"),
            P("dp", None),
            P(),
            P("dp", "tensor"),
            P("dp", "tensor"),
        ),
        out_specs=(
            P("dp", "tensor"),
            P("dp", "tensor"),
            P("dp", "tensor"),
            P("dp", None, None, "tensor"),
            P("dp", None, None, "tensor"),
        ),
        check_vma=False,
    )
```
